256 devices in a mesh: ctx: 4 (over x_lo, core), br: 64 (over x_hi, y, z).
Axes of the slice: x: 4 (x_hi: 2, x_lo: 2; x = x_hi * 2 + x_lo), y: 4, z: 8, core: 2. Of those that a mesh axis runs over, the one named last changes fastest.
Arguments:
- queries: bfloat16 [128, 8192], P('br', 'ctx'), may hold values from -80 to 80
- prefix_keys: bfloat16 [131072, 1024], P(('ctx', 'br')), may hold values from -4 to 4
- prefix_values: bfloat16 [131072, 1024], P(('ctx', 'br')), may hold values from -6 to 6
- branch_suffix_keys: bfloat16 [128, 2048, 1024], P('br', 'ctx'), may hold values from -8 to 8
- suffix_values: bfloat16 [128, 2048, 1024], P('br', 'ctx'), may hold values from -6 to 6
- lengths: int32 [128], P('br'), may hold values from 512 to 2048
Outputs:
- attended: bfloat16 [128, 8192], P('br', 'ctx')
The draws below stay inside these ranges and needn't reach their ends.
All inputs are finite; a program needn't handle non-finite values.
Results may differ from the reference program's by a relative error of at most 0.0045.
Values may be sent and summed in bfloat16 or wider, within the bound.
A program may use at most 64 MiB of HBM per device.

```python
import jax
import jax.numpy as jnp
from jax import lax

H = 64
KEY_VALUE_HEADS = 8
HEAD_SIZE = 128
PRE_DEV = 512
SUFFIX_CAPACITY = 2048
BRANCHES = 128
PREFIX = 131072
N_CTX = 4


def base_keys(key):
    return jnp.clip(jax.random.normal(jax.random.fold_in(key, 11), (PREFIX, KEY_VALUE_HEADS * HEAD_SIZE), jnp.float32), -4.0, 4.0)


def draw_prefix_keys(key, part):
    keys_all = base_keys(key)
    return keys_all.astype(jnp.bfloat16)


def draw_queries(key, part):
    key = jax.random.fold_in(key, 5)
    noise = 3.0 * jnp.clip(jax.random.normal(key, (BRANCHES, H * HEAD_SIZE), jnp.float32), -6.0, 6.0)
    return noise.astype(jnp.bfloat16)


def draw_lengths(key, part):
    key = jax.random.fold_in(key, 7)
    drawn = jax.random.randint(key, (BRANCHES,), SUFFIX_CAPACITY // 4, SUFFIX_CAPACITY + 1, jnp.int32)
    longest = jax.random.randint(jax.random.fold_in(key, 1), (), 0, BRANCHES, jnp.int32)
    return drawn.at[longest].set(SUFFIX_CAPACITY)


def block_levels(key, extent, split, low, top_value):
    def one(position, parts):
        draws = jax.random.uniform(jax.random.fold_in(jax.random.fold_in(key, 6), position), (parts,), jnp.float32, low / len(split), top_value / len(split))
        return jnp.repeat(jnp.exp(draws), extent[position] // parts).reshape((-1,) + (1,) * (len(extent) - position - 1))

    factor_of = one(*split[0])
    for cut in split[1:]:
        factor_of = factor_of * one(*cut)
    return factor_of


def gaussian(rng, extent, deviation, reach, cuts=(), held_as=jnp.bfloat16):
    array = deviation * jax.random.normal(rng, extent, jnp.float32)
    if cuts:
        array = array * block_levels(rng, extent, cuts, -0.22, 0.18)
    return jnp.clip(array, -reach, reach).astype(held_as)


def setup_inputs(seed: int = 0) -> dict:
    arg_keys = jax.random.split(jax.random.key(seed), 7)
    return {
        "queries": draw_queries(jax.random.fold_in(arg_keys[6], 71), 0),
        "prefix_keys": draw_prefix_keys(jax.random.fold_in(arg_keys[6], 71), 0),
        "prefix_values": gaussian(arg_keys[2], (PREFIX, KEY_VALUE_HEADS * HEAD_SIZE), 1.0, 6.0, ((0, 256),)),
        "branch_suffix_keys": gaussian(arg_keys[3], (BRANCHES, SUFFIX_CAPACITY, KEY_VALUE_HEADS * HEAD_SIZE), 1.3, 8.0, ((0, 64), (1, 4))),
        "suffix_values": gaussian(arg_keys[4], (BRANCHES, SUFFIX_CAPACITY, KEY_VALUE_HEADS * HEAD_SIZE), 1.0, 6.0, ((0, 64), (1, 4))),
        "lengths": draw_lengths(jax.random.fold_in(arg_keys[6], 71), 0),
    }


NEG_FILL = -1e30


def head_attention(query_head, prefix_key, prefix_value, suffix_key, suffix_value, live_mask):
    group_size = H // KEY_VALUE_HEADS
    score_scale = HEAD_SIZE ** -0.5
    rollout_branch_count = query_head.shape[0]
    row_count = rollout_branch_count * group_size
    flat_query = query_head.reshape(row_count, HEAD_SIZE)
    block_count = PREFIX // PRE_DEV
    key_blocks = prefix_key.reshape(block_count, PRE_DEV, HEAD_SIZE)
    value_blocks = prefix_value.reshape(block_count, PRE_DEV, HEAD_SIZE)

    def block_step(carry, blocks):
        running, numer, denom = carry
        key_block, value_block = blocks
        scores = jnp.dot(flat_query, key_block.T, preferred_element_type=jnp.float32) * score_scale
        block_top = jnp.max(scores, axis=1)
        weights = jnp.exp(scores - block_top[:, None]).astype(jnp.bfloat16)
        block_numer = jnp.dot(weights, value_block, preferred_element_type=jnp.float32)
        block_denom = jnp.sum(weights.astype(jnp.float32), axis=1)
        newest = jnp.maximum(running, block_top)
        old_factor = jnp.exp(running - newest)
        new_factor = jnp.exp(block_top - newest)
        numer = numer * old_factor[:, None] + block_numer * new_factor[:, None]
        denom = denom * old_factor + block_denom * new_factor
        return (newest, numer, denom), None

    start = (jnp.full((row_count,), NEG_FILL, jnp.float32), jnp.zeros((row_count, HEAD_SIZE), jnp.float32), jnp.zeros((row_count,), jnp.float32))
    (running, numer, denom), _ = lax.scan(block_step, start, (key_blocks, value_blocks))
    segment = SUFFIX_CAPACITY // N_CTX
    suffix_raw = jnp.einsum("bgd,bsd->bgs", query_head.astype(jnp.float32), suffix_key.astype(jnp.float32)) * score_scale
    suffix_raw = jnp.where(live_mask[:, None, :], suffix_raw, NEG_FILL)
    raw_blocks = suffix_raw.reshape(rollout_branch_count, group_size, N_CTX, segment)
    live_blocks = live_mask.reshape(rollout_branch_count, 1, N_CTX, segment)
    suffix_top = jnp.max(raw_blocks, axis=3)
    suffix_weights = jnp.where(live_blocks, jnp.exp(raw_blocks - suffix_top[:, :, :, None]), 0.0).astype(jnp.bfloat16)
    value_split = suffix_value.reshape(rollout_branch_count, N_CTX, segment, HEAD_SIZE).astype(jnp.float32)
    suffix_numer = jnp.einsum("bgcs,bcsd->bgcd", suffix_weights.astype(jnp.float32), value_split)
    suffix_denom = jnp.sum(suffix_weights.astype(jnp.float32), axis=3)
    prefix_top = running.reshape(rollout_branch_count, group_size)
    top_score = jnp.maximum(prefix_top, jnp.max(suffix_top, axis=2))
    prefix_factor = jnp.exp(prefix_top - top_score)
    suffix_factor = jnp.exp(suffix_top - top_score[:, :, None])
    numerator = numer.reshape(rollout_branch_count, group_size, HEAD_SIZE) * prefix_factor[:, :, None] + jnp.sum(suffix_numer * suffix_factor[:, :, :, None], axis=2)
    denominator = denom.reshape(rollout_branch_count, group_size) * prefix_factor + jnp.sum(suffix_denom * suffix_factor, axis=2)
    return numerator / denominator[:, :, None]


def reference(queries, prefix_keys, prefix_values, branch_suffix_keys, suffix_values, lengths):
    group_size = H // KEY_VALUE_HEADS
    rollout_branch_count = queries.shape[0]
    branch_query_heads = queries.reshape(rollout_branch_count, KEY_VALUE_HEADS, group_size, HEAD_SIZE).transpose(1, 0, 2, 3)
    prompt_key_heads = prefix_keys.reshape(PREFIX, KEY_VALUE_HEADS, HEAD_SIZE).transpose(1, 0, 2)
    prompt_value_heads = prefix_values.reshape(PREFIX, KEY_VALUE_HEADS, HEAD_SIZE).transpose(1, 0, 2)
    suffix_key_heads = branch_suffix_keys.reshape(rollout_branch_count, SUFFIX_CAPACITY, KEY_VALUE_HEADS, HEAD_SIZE).transpose(2, 0, 1, 3)
    suffix_value_heads = suffix_values.reshape(rollout_branch_count, SUFFIX_CAPACITY, KEY_VALUE_HEADS, HEAD_SIZE).transpose(2, 0, 1, 3)
    live_mask = jnp.arange(SUFFIX_CAPACITY, dtype=jnp.int32)[None, :] < lengths[:, None]

    def single_head(pieces):
        return head_attention(pieces[0], pieces[1], pieces[2], pieces[3], pieces[4], live_mask)

    attention_output = lax.map(single_head, (branch_query_heads, prompt_key_heads, prompt_value_heads, suffix_key_heads, suffix_value_heads))
    return attention_output.transpose(1, 0, 2, 3).reshape(rollout_branch_count, H * HEAD_SIZE).astype(jnp.bfloat16)
```

```python
import jax
import jax.numpy as jnp
from jax import lax
from jax.experimental import pallas as pl
from jax.experimental.pallas import tpu as pltpu
from jax.sharding import PartitionSpec as P

MESH = pl.DeviceIdType.MESH
BF = jnp.bfloat16
F32 = jnp.float32

D = 128
SPAN = 512
NX, NY, NZ = 4, 4, 8
ROWS = 16
TILE = 144
SCALE = D ** (-0.5)
LOG2E = 1.4426950408889634
C2 = SCALE * LOG2E
NEG = -1e30


def nt(a, b):
    return lax.dot_general(a, b, (((1,), (1,)), ((), ())), preferred_element_type=F32)


def pack(ref, numer, top, denom):
    row = lax.broadcasted_iota(jnp.int32, (16, top.shape[1]), 0)
    high = denom.astype(BF).astype(F32)
    low = denom - high
    stats = jnp.where(row == 0, top, jnp.where(row == 1, high, low))
    ref[0:D, :] = numer.astype(BF)
    ref[D:TILE, :] = stats.astype(BF)


def merge(refs):
    stats = [r[D:TILE, :].astype(F32) for r in refs]
    tops = [s[0:1, :] for s in stats]
    top = tops[0]
    for t in tops[1:]:
        top = jnp.maximum(top, t)
    numer, denom = None, None
    for r, s, t in zip(refs, stats, tops):
        factor = jnp.exp2((t - top) * C2)
        n = r[0:D, :].astype(F32) * factor
        d = (s[1:2, :] + s[2:3, :]) * factor
        numer = n if numer is None else numer + n
        denom = d if denom is None else denom + d
    return numer, top, denom


def kernel(
    len_ref, q_ref, pk, pv, sk, sv, out_ref,
    qscr, qz, qc, q0, q1, kbuf, vbuf, vt, skb, svb, qbd,
    o0, o1, rx0, rx1, m0, m1, ry0, ry1, zb, rz, sb, sr, fs, ft, oscr,
    s1, r1, s2, r2, s3, r3, s4, r4, s5, r5, s6, r6, s7, r7, s8, r8, skv, rkv, loc,
):
    c = lax.axis_index("ctx")
    br = lax.axis_index("br")
    core = c % 2
    xlo = c // 2
    z = br % NZ
    y = (br // NZ) % NY
    xhi = br // (NZ * NY)
    x = xhi * 2 + xlo

    def dev(px, py, pz, pc):
        return ((px % 2) * 2 + pc, (px // 2) * (NZ * NY) + py * NZ + pz)

    def xpeer(i):
        return dev((x + i) % NX, y, z, core)

    def ypeer(i):
        return dev(x, (y + i) % NY, z, core)

    def zpeer(i):
        return dev(x, y, (z + i) % NZ, core)

    def cpeer(i):
        return ((c + i) % 4, br)

    mate = dev(x, y, z, 1 - core)

    def remote(src, dst, ssem, rsem, who):
        return pltpu.make_async_remote_copy(
            src_ref=src, dst_ref=dst, send_sem=ssem, recv_sem=rsem, device_id=who, device_id_type=MESH
        )

    sends = []

    def push(src, dst, ssem, rsem, who):
        copy = remote(src, dst, ssem, rsem, who)
        copy.start()
        sends.append(copy)

    def arrived(dst, ssem, rsem, who):
        remote(dst, dst, ssem, rsem, who).wait_recv()

    local = []

    def load(src, dst):
        copy = pltpu.make_async_copy(src, dst, loc.at[len(local)])
        copy.start()
        local.append(copy)

    def cols(a, k):
        return pl.ds(pl.multiple_of((a * 2 + k) * 256, 256), 256)

    for a in range(2):
        load(pk.at[:, cols(a, core)], kbuf.at[a, 0:SPAN])
        load(pv.at[:, cols(a, core)], vbuf.at[a, 0:SPAN])
    load(sk, skb)
    load(sv, svb)

    qf = q_ref[...].astype(F32)
    for j in range(16):
        qscr[2 * j : 2 * j + 2, :] = qf[:, D * j : D * (j + 1)]
    for k in range(2):
        qk = qscr[ROWS * k : ROWS * (k + 1), :].astype(BF)
        qz[z, k] = qk
        qc[c, k] = qk

    barrier = pltpu.get_barrier_semaphore()
    peers = [zpeer(i) for i in range(1, NZ)] + [ypeer(i) for i in range(1, NY)] + [xpeer(i) for i in range(1, NX)]
    peers += [mate, dev(x + 1 - 2 * xlo, y, z, 1 - core)]
    for who in peers:
        pl.semaphore_signal(barrier, inc=1, device_id=who, device_id_type=MESH)
    pl.semaphore_wait(barrier, len(peers))

    for i in range(1, NZ):
        push(qz.at[z], qz.at[z], s1.at[i], r1.at[i], zpeer(i))
    for i in range(1, 4):
        push(qz.at[z], qc.at[c], s7.at[i], r7.at[i], cpeer(i))
    for a in range(2):
        push(pk.at[:, cols(a, 1 - core)], kbuf.at[a, SPAN : 2 * SPAN], skv.at[a], rkv.at[a], mate)
        push(pv.at[:, cols(a, 1 - core)], vbuf.at[a, SPAN : 2 * SPAN], skv.at[2 + a], rkv.at[2 + a], mate)

    qbd[...] = jnp.zeros_like(qbd)
    fs[...] = jnp.zeros_like(fs)

    for i in range(1, NZ):
        src = (z + NZ - i) % NZ
        arrived(qz.at[src], s1.at[i], r1.at[i], zpeer(i))

    for i in range(1, 4):
        push(qz.at[:, 0], q0.at[x, y], s2.at[0, i], r2.at[0, i], ypeer(i))
        push(qz.at[:, 1], q1.at[y, xlo, xhi], s2.at[1, i], r2.at[1, i], xpeer(i))
    q0[x, y] = qz[:, 0]
    q1[y, xlo, xhi] = qz[:, 1]

    def forward(j):
        py = (y + NY - j) % NY
        px = (x + NX - j) % NX
        for i in range(1, 4):
            push(q0.at[x, py], q0.at[x, py], s3.at[0, j, i], r3.at[0, j, i], xpeer(i))
            t = q1.at[y, px % 2, px // 2]
            push(t, t, s3.at[1, j, i], r3.at[1, j, i], ypeer(i))

    forward(0)

    for i in range(1, 4):
        arrived(qc.at[(c + 4 - i) % 4], s7.at[i], r7.at[i], cpeer(i))
    for h in range(8):
        qbd[ROWS * h : ROWS * (h + 1), D * h : D * (h + 1)] = qc[h // 2, h % 2]
    for copy in local:
        copy.wait()
    raw = jnp.concatenate([nt(qbd[...], skb[0]), nt(qbd[...], skb[1])], axis=1)
    row = lax.broadcasted_iota(jnp.int32, (8 * ROWS, 2 * SPAN), 0)
    col = lax.broadcasted_iota(jnp.int32, (8 * ROWS, 2 * SPAN), 1)
    branch = col // SPAN
    live = (row % 2 == branch) & (c * SPAN + col % SPAN < jnp.where(branch == 0, len_ref[0], len_ref[1]))
    raw = jnp.where(live, raw, NEG)
    stop = jnp.max(raw, axis=1, keepdims=True)
    w = jnp.where(live, jnp.exp2((raw - stop) * C2), 0.0).astype(BF)
    sden = jnp.sum(w.astype(F32), axis=1, keepdims=True)
    snum = jnp.dot(w[:, :SPAN], svb[0], preferred_element_type=F32) + jnp.dot(
        w[:, SPAN:], svb[1], preferred_element_type=F32
    )
    lane = lax.broadcasted_iota(jnp.int32, (8 * ROWS, D), 1)
    sstat = jnp.where(lane == 0, stop, sden)
    for h in range(8):
        r = slice(ROWS * (h % 2), ROWS * (h % 2) + ROWS)
        sb[h // 2, 0, r, :] = snum[ROWS * h : ROWS * (h + 1), D * h : D * (h + 1)]
        sb[h // 2, 1, r, :] = sstat[ROWS * h : ROWS * (h + 1), :]
    for i in range(1, 4):
        push(sb.at[(c + i) % 4], sr.at[i], s8.at[i], r8.at[i], cpeer(i))
    sr[0] = sb[c]

    for j in range(1, 4):
        py = (y + NY - j) % NY
        px = (x + NX - j) % NX
        arrived(q0.at[x, py], s2.at[0, j], r2.at[0, j], ypeer(j))
        arrived(q1.at[y, px % 2, px // 2], s2.at[1, j], r2.at[1, j], xpeer(j))
        forward(j)

    for a in range(2):
        arrived(kbuf.at[a, SPAN : 2 * SPAN], skv.at[a], rkv.at[a], mate)
        arrived(vbuf.at[a, SPAN : 2 * SPAN], skv.at[2 + a], rkv.at[2 + a], mate)
    for a in range(2):
        for k in range(2):
            vt[a, k, 0:D, :] = vbuf[a, :, D * k : D * (k + 1)].T
            vt[a, k, D:TILE, :] = jnp.ones((16, 2 * SPAN), BF)

    def unit(a, k, q, out_a, out_b):
        s = nt(kbuf[a, :, D * k : D * (k + 1)], q)
        top = jnp.max(s, axis=0, keepdims=True).astype(BF).astype(F32)
        p = jnp.exp2((s - top) * C2).astype(BF)
        n = jnp.dot(vt[a, k], p, preferred_element_type=F32)
        den = n[D : D + 1, :]
        pack(out_a, n[0:D, :D], top[:, :D], den[:, :D])
        pack(out_b, n[0:D, D:], top[:, D:], den[:, D:])

    def result(t, p):
        i = t + t // 2 - 2 * (t // 3)
        px = (x + NX - i) % NX
        py = (y + NY - i) % NY
        first = remote(
            o0.at[px, pl.ds(2 * p, 2)], rx0.at[i, pl.ds(2 * p, 2)], s4.at[0, i, p], r4.at[0, i, p],
            dev(px, y, z, core),
        )
        second = remote(
            o1.at[py, p], rx1.at[i, p], s4.at[1, i, p], r4.at[1, i, p], dev(x, py, z, core)
        )
        return i, px, py, first, second

    def step(n, _):
        t, p = n // 2, n % 2
        i, px, py, first, second = result(t, p)

        @pl.when(t > 0)
        def _():
            for e in range(2):
                ty = 2 * p + e
                j = (y + NY - ty) % NY
                arrived(q0.at[px, ty], s3.at[0, j, i], r3.at[0, j, i], dev(px, y, z, core))
                tx = 2 * e + p
                j = (x + NX - tx) % NX
                arrived(q1.at[py, p, e], s3.at[1, j, i], r3.at[1, j, i], dev(x, py, z, core))

        unit(px % 2, 0, q0[px, pl.ds(2 * p, 2)].reshape(256, D), o0.at[px, 2 * p], o0.at[px, 2 * p + 1])
        unit(p, 1, q1[py, p].reshape(256, D), o1.at[py, p, 0], o1.at[py, p, 1])

        @pl.when(t > 0)
        def _():
            first.start()
            second.start()

        return 0

    lax.fori_loop(0, 8, step, 0)

    for i in range(1, 4):
        for p in range(2):
            arrived(rx0.at[i, 2 * p : 2 * p + 2], s4.at[0, i, p], r4.at[0, i, p], xpeer(i))
            arrived(rx1.at[i, p], s4.at[1, i, p], r4.at[1, i, p], ypeer(i))

    for i in (1, 2, 3, 0):
        py = (y + i) % NY
        px = (x + i) % NX
        a, h = px % 2, px // 2
        pack(m0.at[py], *merge([o0.at[x, py]] + [rx0.at[j, py] for j in range(1, 4)]))
        pack(m1.at[a, h], *merge([o1.at[y, a, h]] + [rx1.at[j, a, h] for j in range(1, 4)]))
        if i:
            push(m0.at[py], ry0.at[i], s5.at[0, i], r5.at[0, i], ypeer(i))
            push(m1.at[a, h], ry1.at[i], s5.at[1, i], r5.at[1, i], xpeer(i))
    for i in range(1, 4):
        arrived(ry0.at[i], s5.at[0, i], r5.at[0, i], ypeer(i))
        arrived(ry1.at[i], s5.at[1, i], r5.at[1, i], xpeer(i))
    n0, t0, d0 = merge([m0.at[y]] + [ry0.at[j] for j in range(1, 4)])
    n1, t1, d1 = merge([m1.at[xlo, xhi]] + [ry1.at[j] for j in range(1, 4)])

    zb[:, 0] = n0.T.astype(BF).reshape(NZ, ROWS, D)
    zb[:, 1] = n1.T.astype(BF).reshape(NZ, ROWS, D)
    h0 = d0.astype(BF).astype(F32)
    h1 = d1.astype(BF).astype(F32)
    srow = lax.broadcasted_iota(jnp.int32, (16, D), 0)
    st = jnp.zeros((16, D), F32)
    for n, v in enumerate((t0, h0, d0 - h0, t1, h1, d1 - h1)):
        st = jnp.where(srow == n, v, st)
    st = st.astype(BF)
    for i in range(NZ):
        zb[i, 2] = st
    for i in range(1, NZ):
        push(zb.at[(z + i) % NZ], rz.at[i], s6.at[i], r6.at[i], zpeer(i))
    rz[0] = zb[z]

    for i in range(1, 4):
        arrived(sr.at[i], s8.at[i], r8.at[i], cpeer(i))
    suffix = []
    for k in range(2):
        r = slice(ROWS * k, ROWS * (k + 1))
        tops = [sr[i, 1, r, 0:1] for i in range(4)]
        top = jnp.maximum(jnp.maximum(tops[0], tops[1]), jnp.maximum(tops[2], tops[3]))
        num = jnp.zeros((ROWS, D), F32)
        den = jnp.zeros((ROWS, 1), F32)
        for i in range(4):
            f = jnp.exp2((tops[i] - top) * C2)
            num = num + f * sr[i, 0, r, :]
            den = den + f * sr[i, 1, r, 1:2]
        suffix.append((num, top, den))

    for i in range(1, NZ):
        arrived(rz.at[i], s6.at[i], r6.at[i], zpeer(i))
    stats = [rz[i, 2].astype(F32) for i in range(NZ)]
    for k in range(2):
        tops = [s[3 * k : 3 * k + 1, :] for s in stats]
        top = tops[0]
        for t in tops[1:]:
            top = jnp.maximum(top, t)
        den = jnp.zeros((1, D), F32)
        for i in range(NZ):
            f = jnp.exp2((tops[i] - top) * C2)
            den = den + f * (stats[i][3 * k + 1 : 3 * k + 2, :] + stats[i][3 * k + 2 : 3 * k + 3, :])
            fs[16 * k + i : 16 * k + i + 1, :] = f
        fs[16 * k + 8 : 16 * k + 9, :] = top
        fs[16 * k + 9 : 16 * k + 10, :] = den
    ft[...] = fs[...].T
    own = ft[pl.ds(pl.multiple_of(z * ROWS, ROWS), ROWS), :]
    for k in range(2):
        num = jnp.zeros((ROWS, D), F32)
        for i in range(NZ):
            num = num + own[:, 16 * k + i : 16 * k + i + 1] * rz[i, k].astype(F32)
        top = own[:, 16 * k + 8 : 16 * k + 9]
        den = own[:, 16 * k + 9 : 16 * k + 10]
        snum, stop, sden = suffix[k]
        both = jnp.maximum(top, stop)
        f = jnp.exp2((top - both) * C2)
        g = jnp.exp2((stop - both) * C2)
        att = (num * f + snum * g) / (den * f + sden * g)
        for j in range(8):
            oscr[:, D * (8 * k + j) : D * (8 * k + j + 1)] = att[2 * j : 2 * j + 2, :]
    out_ref[...] = oscr[...].astype(BF)

    for copy in sends:
        copy.wait_send()

    def drain(n, _):
        _, _, _, first, second = result(n // 2, n % 2)
        first.wait_send()
        second.wait_send()
        return 0

    lax.fori_loop(2, 8, drain, 0)


def body(queries, prefix_keys, prefix_values, branch_suffix_keys, suffix_values, lengths):
    dma = pltpu.SemaphoreType.DMA
    vmem = pltpu.VMEM
    scratch = [
        vmem((32, D), F32),
        vmem((NZ, 2, ROWS, D), BF),
        vmem((4, 2, ROWS, D), BF),
        vmem((NX, NY, NZ, ROWS, D), BF),
        vmem((NY, 2, 2, NZ, ROWS, D), BF),
        vmem((2, 2 * SPAN, 256), BF),
        vmem((2, 2 * SPAN, 256), BF),
        vmem((2, 2, TILE, 2 * SPAN), BF),
        vmem((2, SPAN, 1024), BF),
        vmem((2, SPAN, 1024), BF),
        vmem((128, 1024), BF),
        vmem((NX, NY, TILE, D), BF),
        vmem((NY, 2, 2, TILE, D), BF),
        vmem((4, NY, TILE, D), BF),
        vmem((4, 2, 2, TILE, D), BF),
        vmem((NY, TILE, D), BF),
        vmem((2, 2, TILE, D), BF),
        vmem((4, TILE, D), BF),
        vmem((4, TILE, D), BF),
        vmem((NZ, 3, ROWS, D), BF),
        vmem((NZ, 3, ROWS, D), BF),
        vmem((4, 2, 32, D), F32),
        vmem((4, 2, 32, D), F32),
        vmem((D, D), F32),
        vmem((D, D), F32),
        vmem((2, 2048), F32),
        dma((8,)), dma((8,)),
        dma((2, 4)), dma((2, 4)),
        dma((2, 4, 4)), dma((2, 4, 4)),
        dma((2, 4, 2)), dma((2, 4, 2)),
        dma((2, 4)), dma((2, 4)),
        dma((8,)), dma((8,)),
        dma((4,)), dma((4,)),
        dma((4,)), dma((4,)),
        dma((4,)), dma((4,)),
        dma((6,)),
    ]
    hbm = pl.BlockSpec(memory_space=pl.ANY)
    return pl.pallas_call(
        kernel,
        out_shape=jax.ShapeDtypeStruct((2, 2048), BF),
        in_specs=[
            pl.BlockSpec(memory_space=pltpu.SMEM),
            pl.BlockSpec(memory_space=pltpu.VMEM),
            hbm, hbm, hbm, hbm,
        ],
        out_specs=pl.BlockSpec(memory_space=pltpu.VMEM),
        scratch_shapes=scratch,
        compiler_params=pltpu.CompilerParams(
            collective_id=0, has_side_effects=True, vmem_limit_bytes=48 * 1024 * 1024
        ),
        cost_estimate=pl.CostEstimate(flops=2_800_000_000, bytes_accessed=8_000_000, transcendentals=4_500_000),
        name="attend",
    )(lengths, queries, prefix_keys, prefix_values, branch_suffix_keys, suffix_values)


def solution(mesh):
    placed = (
        P("br", "ctx"),
        P(("ctx", "br"), None),
        P(("ctx", "br"), None),
        P("br", "ctx", None),
        P("br", "ctx", None),
        P("br"),
    )
    return jax.shard_map(
        body, mesh=mesh, in_specs=placed, out_specs=P("br", "ctx"), check_vma=False
    )
```

```python
import functools

import jax
import jax.numpy as jnp
from jax import lax
from jax.experimental import pallas as pl
from jax.experimental.pallas import tpu as pltpu
from jax.sharding import PartitionSpec as P

MESH = pl.DeviceIdType.MESH
BF = jnp.bfloat16
F32 = jnp.float32

D = 128
SPAN = 512
NX, NY, NZ = 4, 4, 8
ROWS = 16
TILE = 144
SCALE = D ** (-0.5)
LOG2E = 1.4426950408889634
C2 = SCALE * LOG2E
NEG = -1e30
CHUNK = 256


def nt(a, b):
    return lax.dot_general(a, b, (((1,), (1,)), ((), ())), preferred_element_type=F32)


def pack(ref, numer, top, denom):
    row = lax.broadcasted_iota(jnp.int32, (16, top.shape[1]), 0)
    high = denom.astype(BF).astype(F32)
    low = denom - high
    stats = jnp.where(row == 0, top, jnp.where(row == 1, high, low))
    ref[0:D, :] = numer.astype(BF)
    ref[D:TILE, :] = stats.astype(BF)


def merge(refs):
    stats = [r[D:TILE, :].astype(F32) for r in refs]
    tops = [s[0:1, :] for s in stats]
    top = tops[0]
    for t in tops[1:]:
        top = jnp.maximum(top, t)
    numer, denom = None, None
    for r, s, t in zip(refs, stats, tops):
        factor = jnp.exp2((t - top) * C2)
        n = r[0:D, :].astype(F32) * factor
        d = (s[1:2, :] + s[2:3, :]) * factor
        numer = n if numer is None else numer + n
        denom = d if denom is None else denom + d
    return numer, top, denom


def kernel(
    len_ref, q_ref, pk, pv, sk, sv, out_ref,
    qraw, qscr, qz, qc, q0, q1, kbuf, vbuf, vt, skb, svb, qbd, ss, ps,
    o0, o1, rx0, rx1, m0, m1, ry0, ry1, zb, rz, sb, sr, fs, ft, oscr,
    s1, r1, s2, r2, s3, r3, s4, r4, s5, r5, s6, r6, s7, r7, s8, r8, skv, rkv, loc,
):
    c = lax.axis_index("ctx")
    br = lax.axis_index("br")
    core = c % 2
    xlo = c // 2
    z = br % NZ
    y = (br // NZ) % NY
    xhi = br // (NZ * NY)
    x = xhi * 2 + xlo

    def dev(px, py, pz, pc):
        return ((px % 2) * 2 + pc, (px // 2) * (NZ * NY) + py * NZ + pz)

    def xpeer(i):
        return dev((x + i) % NX, y, z, core)

    def ypeer(i):
        return dev(x, (y + i) % NY, z, core)

    def zpeer(i):
        return dev(x, y, (z + i) % NZ, core)

    def cpeer(i):
        return ((c + i) % 4, br)

    mate = dev(x, y, z, 1 - core)

    def remote(src, dst, ssem, rsem, who):
        return pltpu.make_async_remote_copy(
            src_ref=src, dst_ref=dst, send_sem=ssem, recv_sem=rsem, device_id=who, device_id_type=MESH
        )

    sends = []

    def push(src, dst, ssem, rsem, who):
        copy = remote(src, dst, ssem, rsem, who)
        copy.start()
        sends.append(copy)

    def arrived(dst, ssem, rsem, who):
        remote(dst, dst, ssem, rsem, who).wait_recv()

    local = []

    def load(src, dst):
        copy = pltpu.make_async_copy(src, dst, loc.at[len(local)])
        copy.start()
        local.append(copy)

    def cols(a, k):
        return pl.ds(pl.multiple_of((a * 2 + k) * 256, 256), 256)

    barrier = pltpu.get_barrier_semaphore()
    peers = [zpeer(i) for i in range(1, NZ)] + [ypeer(i) for i in range(1, NY)] + [xpeer(i) for i in range(1, NX)]
    peers += [mate, dev(x + 1 - 2 * xlo, y, z, 1 - core)]
    for who in peers:
        pl.semaphore_signal(barrier, inc=1, device_id=who, device_id_type=MESH)

    load(q_ref, qraw)
    for a in range(2):
        load(pk.at[:, cols(a, core)], kbuf.at[a, 0:SPAN])
        load(pv.at[:, cols(a, core)], vbuf.at[a, 0:SPAN])
    load(sk, skb)
    load(sv, svb)

    local.pop(0).wait()
    qf = qraw[...].astype(F32)
    for j in range(16):
        qscr[2 * j : 2 * j + 2, :] = qf[:, D * j : D * (j + 1)]
    for k in range(2):
        qk = qscr[ROWS * k : ROWS * (k + 1), :].astype(BF)
        qz[z, k] = qk
        qc[c, k] = qk

    qbd[...] = jnp.zeros_like(qbd)
    fs[...] = jnp.zeros_like(fs)

    def turn(a, k, part):
        vt[a, k, 0:D, SPAN * part : SPAN * (part + 1)] = vbuf[
            a, SPAN * part : SPAN * (part + 1), D * k : D * (k + 1)
        ].T

    for copy in local[:4]:
        copy.wait()
    for a in range(2):
        for k in range(2):
            turn(a, k, 0)
            vt[a, k, D:TILE, :] = jnp.ones((16, 2 * SPAN), BF)

    pl.semaphore_wait(barrier, len(peers))

    for i in range(1, NZ):
        push(qz.at[z], qz.at[z], s1.at[i], r1.at[i], zpeer(i))
    for i in range(1, 4):
        push(qz.at[z], qc.at[c], s7.at[i], r7.at[i], cpeer(i))
    for a in range(2):
        push(pk.at[:, cols(a, 1 - core)], kbuf.at[a, SPAN : 2 * SPAN], skv.at[a], rkv.at[a], mate)
        push(pv.at[:, cols(a, 1 - core)], vbuf.at[a, SPAN : 2 * SPAN], skv.at[2 + a], rkv.at[2 + a], mate)

    for i in range(1, NZ):
        src = (z + NZ - i) % NZ
        arrived(qz.at[src], s1.at[i], r1.at[i], zpeer(i))

    for i in range(1, 4):
        push(qz.at[:, 0], q0.at[y, xlo, xhi], s2.at[0, i], r2.at[0, i], ypeer(i))
        push(qz.at[:, 1], q1.at[x, y], s2.at[1, i], r2.at[1, i], xpeer(i))
    q0[y, xlo, xhi] = qz[:, 0]
    q1[x, y] = qz[:, 1]

    def forward(j):
        t0 = q0.at[(y + NY - j) % NY, xlo, xhi]
        t1 = q1.at[(x + NX - j) % NX, y]
        for i in range(1, 4):
            push(t0, t0, s3.at[0, j, i], r3.at[0, j, i], xpeer(i))
            push(t1, t1, s3.at[1, j, i], r3.at[1, j, i], ypeer(i))

    forward(0)

    for i in range(1, 4):
        arrived(qc.at[(c + 4 - i) % 4], s7.at[i], r7.at[i], cpeer(i))
    for h in range(8):
        qbd[ROWS * h : ROWS * (h + 1), D * h : D * (h + 1)] = qc[h // 2, h % 2]
    for copy in local[4:]:
        copy.wait()
    raw = jnp.concatenate([nt(qbd[...], skb[0]), nt(qbd[...], skb[1])], axis=1)
    row = lax.broadcasted_iota(jnp.int32, (8 * ROWS, 2 * SPAN), 0)
    col = lax.broadcasted_iota(jnp.int32, (8 * ROWS, 2 * SPAN), 1)
    branch = col // SPAN
    live = (row % 2 == branch) & (c * SPAN + col % SPAN < jnp.where(branch == 0, len_ref[0], len_ref[1]))
    raw = jnp.where(live, raw, NEG)
    stop = jnp.max(raw, axis=1, keepdims=True)
    w = jnp.where(live, jnp.exp2((raw - stop) * C2), 0.0).astype(BF)
    sden = jnp.sum(w.astype(F32), axis=1, keepdims=True)
    snum = jnp.dot(w[:, :SPAN], svb[0], preferred_element_type=F32) + jnp.dot(
        w[:, SPAN:], svb[1], preferred_element_type=F32
    )
    lane = lax.broadcasted_iota(jnp.int32, (8 * ROWS, D), 1)
    sstat = jnp.where(lane == 0, stop, sden)
    for h in range(8):
        r = slice(ROWS * (h % 2), ROWS * (h % 2) + ROWS)
        sb[h // 2, 0, r, :] = snum[ROWS * h : ROWS * (h + 1), D * h : D * (h + 1)]
        sb[h // 2, 1, r, :] = sstat[ROWS * h : ROWS * (h + 1), :]
    for i in range(1, 4):
        push(sb.at[(c + i) % 4], sr.at[i], s8.at[i], r8.at[i], cpeer(i))
    sr[0] = sb[c]

    for j in range(1, 4):
        arrived(q0.at[(y + NY - j) % NY, xlo, xhi], s2.at[0, j], r2.at[0, j], ypeer(j))
        arrived(q1.at[(x + NX - j) % NX, y], s2.at[1, j], r2.at[1, j], xpeer(j))
        forward(j)

    for a in range(2):
        arrived(kbuf.at[a, SPAN : 2 * SPAN], skv.at[a], rkv.at[a], mate)
        arrived(vbuf.at[a, SPAN : 2 * SPAN], skv.at[2 + a], rkv.at[2 + a], mate)
    for a in range(2):
        for k in range(2):
            turn(a, k, 1)

    def attend(units, after):
        def score(u, n):
            a, k, q = units[u][:3]
            rows = slice(CHUNK * n, CHUNK * (n + 1))
            s = nt(kbuf[a, rows, D * k : D * (k + 1)], q)
            ss[u % 2, rows] = s
            return jnp.max(s, axis=0, keepdims=True)

        count = 2 * SPAN // CHUNK
        tops = [score(0, n) for n in range(count)]
        for u, (a, k, _, out_a, out_b) in enumerate(units):
            top = functools.reduce(jnp.maximum, tops).astype(BF).astype(F32)
            tops = []
            for n in range(count):
                if u + 1 < len(units):
                    tops.append(score(u + 1, n))
                rows = slice(CHUNK * n, CHUNK * (n + 1))
                ps[u % 2, rows] = jnp.exp2((ss[u % 2, rows] - top) * C2).astype(BF)
            n = jnp.dot(vt[a, k], ps[u % 2], preferred_element_type=F32)
            den = n[D : D + 1, :]
            pack(out_a, n[0:D, :D], top[:, :D], den[:, :D])
            pack(out_b, n[0:D, D:], top[:, D:], den[:, D:])
            after(u)

    def partial0(j, i):
        px = (x + i) % NX
        return remote(o0.at[j, px % 2, px // 2], rx0.at[i, j], s4.at[0, j, i], r4.at[0, j, i], xpeer(i))

    def partial1(j, i):
        return remote(o1.at[j, (y + i) % NY], rx1.at[i, j], s4.at[1, j, i], r4.at[1, j, i], ypeer(i))

    def sums(j):
        return (
            remote(m0.at[j], ry0.at[j], s5.at[0, j], r5.at[0, j], ypeer(NY - j)),
            remote(m1.at[j], ry1.at[j], s5.at[1, j], r5.at[1, j], xpeer(NX - j)),
        )

    def reduce(j):
        for i in range(1, 4):
            partial0(j, i).wait_recv()
        pack(m0.at[j], *merge([o0.at[j, xlo, xhi]] + [rx0.at[i, j] for i in range(1, 4)]))
        for i in range(1, 4):
            partial1(j, i).wait_recv()
        pack(m1.at[j], *merge([o1.at[j, y]] + [rx1.at[i, j] for i in range(1, 4)]))

    def step(j, _):
        py = (y + NY - j) % NY
        px = (x + NX - j) % NX
        for i in range(1, 4):
            arrived(q0.at[py, xlo, xhi], s3.at[0, j, i], r3.at[0, j, i], xpeer(i))
            arrived(q1.at[px, y], s3.at[1, j, i], r3.at[1, j, i], ypeer(i))
        units = [(a, 0, q0[py, a].reshape(256, D), o0.at[j, a, 0], o0.at[j, a, 1]) for a in range(2)]
        for v in range(2):
            q = q1[px, 2 * v : 2 * v + 2].reshape(256, D)
            units.append((px % 2, 1, q, o1.at[j, 2 * v], o1.at[j, 2 * v + 1]))

        def after(u):
            for i in range(1, 4):
                if u == 1:
                    partial0(j, i).start()
                if u == 3:
                    partial1(j, i).start()

        attend(units, after)

        @pl.when(j > 0)
        def _():
            reduce(j - 1)

        @pl.when(j > 1)
        def _():
            for copy in sums(j - 1):
                copy.start()

        return 0

    lax.fori_loop(0, 4, step, 0)
    reduce(3)
    for copy in sums(3):
        copy.start()

    for j in range(1, 4):
        for copy in sums(j):
            copy.wait_recv()
    n0, t0, d0 = merge([m0.at[0]] + [ry0.at[j] for j in range(1, 4)])
    n1, t1, d1 = merge([m1.at[0]] + [ry1.at[j] for j in range(1, 4)])

    zb[:, 0] = n0.T.astype(BF).reshape(NZ, ROWS, D)
    zb[:, 1] = n1.T.astype(BF).reshape(NZ, ROWS, D)
    h0 = d0.astype(BF).astype(F32)
    h1 = d1.astype(BF).astype(F32)
    srow = lax.broadcasted_iota(jnp.int32, (16, D), 0)
    st = jnp.zeros((16, D), F32)
    for n, v in enumerate((t0, h0, d0 - h0, t1, h1, d1 - h1)):
        st = jnp.where(srow == n, v, st)
    st = st.astype(BF)
    for i in range(NZ):
        zb[i, 2] = st
    for i in range(1, NZ):
        push(zb.at[(z + i) % NZ], rz.at[i], s6.at[i], r6.at[i], zpeer(i))
    rz[0] = zb[z]

    for i in range(1, 4):
        arrived(sr.at[i], s8.at[i], r8.at[i], cpeer(i))
    suffix = []
    for k in range(2):
        r = slice(ROWS * k, ROWS * (k + 1))
        tops = [sr[i, 1, r, 0:1] for i in range(4)]
        top = jnp.maximum(jnp.maximum(tops[0], tops[1]), jnp.maximum(tops[2], tops[3]))
        num = jnp.zeros((ROWS, D), F32)
        den = jnp.zeros((ROWS, 1), F32)
        for i in range(4):
            f = jnp.exp2((tops[i] - top) * C2)
            num = num + f * sr[i, 0, r, :]
            den = den + f * sr[i, 1, r, 1:2]
        suffix.append((num, top, den))

    for i in range(1, NZ):
        arrived(rz.at[i], s6.at[i], r6.at[i], zpeer(i))
    stats = [rz[i, 2].astype(F32) for i in range(NZ)]
    for k in range(2):
        tops = [s[3 * k : 3 * k + 1, :] for s in stats]
        top = tops[0]
        for t in tops[1:]:
            top = jnp.maximum(top, t)
        den = jnp.zeros((1, D), F32)
        for i in range(NZ):
            f = jnp.exp2((tops[i] - top) * C2)
            den = den + f * (stats[i][3 * k + 1 : 3 * k + 2, :] + stats[i][3 * k + 2 : 3 * k + 3, :])
            fs[16 * k + i : 16 * k + i + 1, :] = f
        fs[16 * k + 8 : 16 * k + 9, :] = top
        fs[16 * k + 9 : 16 * k + 10, :] = den
    ft[...] = fs[...].T
    own = ft[pl.ds(pl.multiple_of(z * ROWS, ROWS), ROWS), :]
    for k in range(2):
        num = jnp.zeros((ROWS, D), F32)
        for i in range(NZ):
            num = num + own[:, 16 * k + i : 16 * k + i + 1] * rz[i, k].astype(F32)
        top = own[:, 16 * k + 8 : 16 * k + 9]
        den = own[:, 16 * k + 9 : 16 * k + 10]
        snum, stop, sden = suffix[k]
        both = jnp.maximum(top, stop)
        f = jnp.exp2((top - both) * C2)
        g = jnp.exp2((stop - both) * C2)
        att = (num * f + snum * g) / (den * f + sden * g)
        for j in range(8):
            oscr[:, D * (8 * k + j) : D * (8 * k + j + 1)] = att[2 * j : 2 * j + 2, :]
    out_ref[...] = oscr[...].astype(BF)

    for copy in sends:
        copy.wait_send()

    def drain(j, _):
        for i in range(1, 4):
            partial0(j, i).wait_send()
            partial1(j, i).wait_send()
        return 0

    lax.fori_loop(0, 4, drain, 0)
    for j in range(1, 4):
        for copy in sums(j):
            copy.wait_send()


def body(queries, prefix_keys, prefix_values, branch_suffix_keys, suffix_values, lengths):
    dma = pltpu.SemaphoreType.DMA
    vmem = pltpu.VMEM
    scratch = [
        vmem((2, 2048), BF),
        vmem((32, D), F32),
        vmem((NZ, 2, ROWS, D), BF),
        vmem((4, 2, ROWS, D), BF),
        vmem((NY, 2, 2, NZ, ROWS, D), BF),
        vmem((NX, NY, NZ, ROWS, D), BF),
        vmem((2, 2 * SPAN, 256), BF),
        vmem((2, 2 * SPAN, 256), BF),
        vmem((2, 2, TILE, 2 * SPAN), BF),
        vmem((2, SPAN, 1024), BF),
        vmem((2, SPAN, 1024), BF),
        vmem((128, 1024), BF),
        vmem((2, 2 * SPAN, 256), F32),
        vmem((2, 2 * SPAN, 256), BF),
        vmem((4, 2, 2, TILE, D), BF),
        vmem((4, NY, TILE, D), BF),
        vmem((4, 4, TILE, D), BF),
        vmem((4, 4, TILE, D), BF),
        vmem((4, TILE, D), BF),
        vmem((4, TILE, D), BF),
        vmem((4, TILE, D), BF),
        vmem((4, TILE, D), BF),
        vmem((NZ, 3, ROWS, D), BF),
        vmem((NZ, 3, ROWS, D), BF),
        vmem((4, 2, 32, D), F32),
        vmem((4, 2, 32, D), F32),
        vmem((D, D), F32),
        vmem((D, D), F32),
        vmem((2, 2048), F32),
        dma((8,)), dma((8,)),
        dma((2, 4)), dma((2, 4)),
        dma((2, 4, 4)), dma((2, 4, 4)),
        dma((2, 4, 4)), dma((2, 4, 4)),
        dma((2, 4)), dma((2, 4)),
        dma((8,)), dma((8,)),
        dma((4,)), dma((4,)),
        dma((4,)), dma((4,)),
        dma((4,)), dma((4,)),
        dma((7,)),
    ]
    hbm = pl.BlockSpec(memory_space=pltpu.HBM)
    return pl.pallas_call(
        kernel,
        out_shape=jax.ShapeDtypeStruct((2, 2048), BF),
        in_specs=[
            pl.BlockSpec(memory_space=pltpu.SMEM),
            hbm, hbm, hbm, hbm, hbm,
        ],
        out_specs=pl.BlockSpec(memory_space=pltpu.VMEM),
        scratch_shapes=scratch,
        compiler_params=pltpu.CompilerParams(
            collective_id=0, has_side_effects=True, vmem_limit_bytes=60 * 1024 * 1024
        ),
        cost_estimate=pl.CostEstimate(flops=2_800_000_000, bytes_accessed=8_000_000, transcendentals=4_500_000),
        name="attend",
    )(lengths, queries, prefix_keys, prefix_values, branch_suffix_keys, suffix_values)


def solution(mesh):
    placed = (
        P("br", "ctx"),
        P(("ctx", "br"), None),
        P(("ctx", "br"), None),
        P("br", "ctx", None),
        P("br", "ctx", None),
        P("br"),
    )
    return jax.shard_map(
        body, mesh=mesh, in_specs=placed, out_specs=P("br", "ctx"), check_vma=False
    )
```

```python
import functools

import jax
import jax.numpy as jnp
from jax import lax
from jax.experimental import pallas as pl
from jax.experimental.pallas import tpu as pltpu
from jax.sharding import PartitionSpec as P

MESH = pl.DeviceIdType.MESH
BF = jnp.bfloat16
F32 = jnp.float32

D = 128
SPAN = 512
NX, NY, NZ = 4, 4, 8
ROWS = 16
TILE = 144
SCALE = D ** (-0.5)
LOG2E = 1.4426950408889634
C2 = SCALE * LOG2E
NEG = -1e30
LAST = 3
CHUNK = 256


def nt(a, b):
    return lax.dot_general(a, b, (((1,), (1,)), ((), ())), preferred_element_type=F32)


def pack(ref, numer, top, denom):
    row = lax.broadcasted_iota(jnp.int32, (16, top.shape[1]), 0)
    high = denom.astype(BF).astype(F32)
    low = denom - high
    stats = jnp.where(row == 0, top, jnp.where(row == 1, high, low))
    ref[0:D, :] = numer.astype(BF)
    ref[D:TILE, :] = stats.astype(BF)


def merge(refs):
    stats = [r[D:TILE, :].astype(F32) for r in refs]
    tops = [s[0:1, :] for s in stats]
    top = tops[0]
    for t in tops[1:]:
        top = jnp.maximum(top, t)
    numer, denom = None, None
    for r, s, t in zip(refs, stats, tops):
        factor = jnp.exp2((t - top) * C2)
        n = r[0:D, :].astype(F32) * factor
        d = (s[1:2, :] + s[2:3, :]) * factor
        numer = n if numer is None else numer + n
        denom = d if denom is None else denom + d
    return numer, top, denom


def kernel(
    len_ref, q_ref, pk, pv, sk, sv, out_ref,
    qraw, qscr, qz, qc, q0, q1, kbuf, vbuf, vt, skb, svb, qbd, ss, ps, pad,
    o0, o1, rx0, rx1, m0, m1, ry0, ry1, zb, rz, sb, sr, fs, ft, oscr,
    sent, rz1, rq2, rq3, rp4, rp5, rp6, rctx, rsuf, rkv, loc,
):
    c = lax.axis_index("ctx")
    br = lax.axis_index("br")
    core = c % 2
    xlo = c // 2
    z = br % NZ
    y = (br // NZ) % NY
    xhi = br // (NZ * NY)
    x = xhi * 2 + xlo

    def dev(px, py, pz, pc):
        return ((px % 2) * 2 + pc, (px // 2) * (NZ * NY) + py * NZ + pz)

    def xpeer(i):
        return dev((x + i) % NX, y, z, core)

    def ypeer(i):
        return dev(x, (y + i) % NY, z, core)

    def zpeer(i):
        return dev(x, y, (z + i) % NZ, core)

    def cpeer(i):
        return ((c + i) % 4, br)

    mate = dev(x, y, z, 1 - core)

    def remote(src, dst, ssem, rsem, who):
        return pltpu.make_async_remote_copy(
            src_ref=src, dst_ref=dst, send_sem=ssem, recv_sem=rsem, device_id=who, device_id_type=MESH
        )

    def push(src, dst, phase, rsem, who):
        remote(src, dst, sent.at[phase], rsem, who).start()

    def take(sem, kib):
        size = pad.at[0 : kib // 4]
        pltpu.make_async_copy(size, size, sem).wait()

    def load(src, dst, n):
        pltpu.make_async_copy(src, dst, loc.at[n]).start()

    def cols(a, k):
        return pl.ds(pl.multiple_of((a * 2 + k) * 256, 256), 256)

    barrier = pltpu.get_barrier_semaphore()
    peers = [zpeer(i) for i in range(1, NZ)] + [ypeer(i) for i in range(1, NY)] + [xpeer(i) for i in range(1, NX)]
    peers += [mate, dev(x + 1 - 2 * xlo, y, z, 1 - core)]
    for who in peers:
        pl.semaphore_signal(barrier, inc=1, device_id=who, device_id_type=MESH)

    load(q_ref, qraw, 0)
    for a in range(2):
        load(pv.at[:, cols(a, core)], vbuf.at[a, 0:SPAN], 1)
        load(pk.at[:, cols(a, core)], kbuf.at[a, 0:SPAN], 2)
    load(sk, skb, 3)
    load(sv, svb, 4)

    pltpu.make_async_copy(qraw, qraw, loc.at[0]).wait()
    qf = qraw[...].astype(F32)
    for j in range(16):
        qscr[2 * j : 2 * j + 2, :] = qf[:, D * j : D * (j + 1)]
    for k in range(2):
        qk = qscr[ROWS * k : ROWS * (k + 1), :].astype(BF)
        qz[z, k] = qk
        qc[c, k] = qk

    qbd[...] = jnp.zeros_like(qbd)
    fs[...] = jnp.zeros_like(fs)

    def turn(a, k, part):
        vt[a, k, 0:D, SPAN * part : SPAN * (part + 1)] = vbuf[
            a, SPAN * part : SPAN * (part + 1), D * k : D * (k + 1)
        ].T

    take(loc.at[1], 512)
    for a in range(2):
        for k in range(2):
            turn(a, k, 0)
            vt[a, k, D:TILE, :] = jnp.ones((16, 2 * SPAN), BF)

    pl.semaphore_wait(barrier, len(peers))

    for i in range(1, NZ):
        push(qz.at[z], qz.at[z], 0, rz1.at[0], zpeer(i))
    for i in range(1, 4):
        push(qz.at[z], qc.at[c], 1, rctx.at[0], cpeer(i))
    for a in range(2):
        push(pk.at[:, cols(a, 1 - core)], kbuf.at[a, SPAN : 2 * SPAN], 2, rkv.at[0], mate)
        push(pv.at[:, cols(a, 1 - core)], vbuf.at[a, SPAN : 2 * SPAN], 2, rkv.at[0], mate)

    take(rz1.at[0], 56)

    for i in range(1, 4):
        push(qz.at[:, 0], q0.at[y, xlo, xhi], 3, rq2.at[i], ypeer(i))
        push(qz.at[:, 1], q1.at[x, y], 3, rq2.at[i], xpeer(i))
    q0[y, xlo, xhi] = qz[:, 0]
    q1[x, y] = qz[:, 1]

    def forward(j):
        t0 = q0.at[(y + NY - j) % NY, xlo, xhi]
        t1 = q1.at[(x + NX - j) % NX, y]
        for i in range(1, 4):
            push(t0, t0, 4, rq3.at[0, j], xpeer(i))
            push(t1, t1, 4, rq3.at[1, j], ypeer(i))

    forward(0)

    take(rctx.at[0], 24)
    for h in range(8):
        qbd[ROWS * h : ROWS * (h + 1), D * h : D * (h + 1)] = qc[h // 2, h % 2]
    pltpu.make_async_copy(skb, skb, loc.at[3]).wait()
    pltpu.make_async_copy(svb, svb, loc.at[4]).wait()
    raw = jnp.concatenate([nt(qbd[...], skb[0]), nt(qbd[...], skb[1])], axis=1)
    row = lax.broadcasted_iota(jnp.int32, (8 * ROWS, 2 * SPAN), 0)
    col = lax.broadcasted_iota(jnp.int32, (8 * ROWS, 2 * SPAN), 1)
    branch = col // SPAN
    live = (row % 2 == branch) & (c * SPAN + col % SPAN < jnp.where(branch == 0, len_ref[0], len_ref[1]))
    raw = jnp.where(live, raw, NEG)
    stop = jnp.max(raw, axis=1, keepdims=True)
    w = jnp.where(live, jnp.exp2((raw - stop) * C2), 0.0).astype(BF)
    sden = jnp.sum(w.astype(F32), axis=1, keepdims=True)
    snum = jnp.dot(w[:, :SPAN], svb[0], preferred_element_type=F32) + jnp.dot(
        w[:, SPAN:], svb[1], preferred_element_type=F32
    )
    lane = lax.broadcasted_iota(jnp.int32, (8 * ROWS, D), 1)
    sstat = jnp.where(lane == 0, stop, sden)
    for h in range(8):
        r = slice(ROWS * (h % 2), ROWS * (h % 2) + ROWS)
        sb[h // 2, 0, r, :] = snum[ROWS * h : ROWS * (h + 1), D * h : D * (h + 1)]
        sb[h // 2, 1, r, :] = sstat[ROWS * h : ROWS * (h + 1), :]
    for i in range(1, 4):
        push(sb.at[(c + i) % 4], sr.at[i], 5, rsuf.at[0], cpeer(i))
    sr[0] = sb[c]

    for j in range(1, 4):
        take(rq2.at[j], 64)
        forward(j)

    take(loc.at[2], 512)
    take(rkv.at[0], 1024)
    for a in range(2):
        for k in range(2):
            turn(a, k, 1)

    def attend(units, after):
        def score(u, n):
            a, k, q = units[u][:3]
            rows = slice(CHUNK * n, CHUNK * (n + 1))
            s = nt(kbuf[a, rows, D * k : D * (k + 1)], q)
            ss[u % 2, rows] = s
            return jnp.max(s, axis=0, keepdims=True)

        count = 2 * SPAN // CHUNK
        tops = [score(0, n) for n in range(count)]
        for u, (a, k, _, out_a, out_b) in enumerate(units):
            top = functools.reduce(jnp.maximum, tops).astype(BF).astype(F32)
            tops = []
            for n in range(count):
                if u + 1 < len(units):
                    tops.append(score(u + 1, n))
                rows = slice(CHUNK * n, CHUNK * (n + 1))
                ps[u % 2, rows] = jnp.exp2((ss[u % 2, rows] - top) * C2).astype(BF)
            n = jnp.dot(vt[a, k], ps[u % 2], preferred_element_type=F32)
            den = n[D : D + 1, :]
            pack(out_a, n[0:D, :D], top[:, :D], den[:, :D])
            pack(out_b, n[0:D, D:], top[:, D:], den[:, D:])
            after(u)

    def partial(j, i):
        px = (x + i) % NX
        py = (y + i) % NY
        mine0 = o0.at[j, px % 2, px // 2]
        mine1 = o1.at[j, py]
        if isinstance(j, int) and j == LAST:
            to0, to1 = dev(px, (y + NY - j) % NY, z, core), dev((x + NX - j) % NX, py, z, core)
        else:
            to0, to1 = xpeer(i), ypeer(i)
        return (
            remote(mine0, rx0.at[i, j], sent.at[6], rp4.at[0, j], to0),
            remote(mine1, rx1.at[i, j], sent.at[6], rp4.at[1, j], to1),
        )

    def reduce(j):
        take(rp4.at[0, j], 108)
        pack(m0.at[j], *merge([o0.at[j, xlo, xhi]] + [rx0.at[i, j] for i in range(1, 4)]))
        take(rp4.at[1, j], 108)
        pack(m1.at[j], *merge([o1.at[j, y]] + [rx1.at[i, j] for i in range(1, 4)]))

    def step(j, _):
        py = (y + NY - j) % NY
        px = (x + NX - j) % NX
        take(rq3.at[0, j], 96)
        take(rq3.at[1, j], 96)
        units = [(a, 0, q0[py, a].reshape(256, D), o0.at[j, a, 0], o0.at[j, a, 1]) for a in range(2)]
        for v in range(2):
            q = q1[px, 2 * v : 2 * v + 2].reshape(256, D)
            units.append((px % 2, 1, q, o1.at[j, 2 * v], o1.at[j, 2 * v + 1]))

        first = 0 if isinstance(j, int) else 1

        def after(u):
            if u % 2:
                for i in range(first, 4):
                    partial(j, i)[u // 2].start()

        attend(units, after)

        @pl.when(j > 0)
        def _():
            reduce(j - 1)

        @pl.when(j > 1)
        def _():
            push(m0.at[j - 1], ry0.at[j - 1], 7, rp5.at[0], ypeer(NY - j + 1))
            push(m1.at[j - 1], ry1.at[j - 1], 7, rp5.at[1], xpeer(NX - j + 1))

        return 0

    lax.fori_loop(0, LAST, step, 0)
    step(LAST, 0)
    take(rp5.at[0], 72)
    take(rp4.at[0, LAST], 144)
    n0, t0, d0 = merge([m0.at[0], ry0.at[1], ry0.at[2]] + [rx0.at[i, LAST] for i in range(4)])
    take(rp5.at[1], 72)
    take(rp4.at[1, LAST], 144)
    n1, t1, d1 = merge([m1.at[0], ry1.at[1], ry1.at[2]] + [rx1.at[i, LAST] for i in range(4)])

    zb[:, 0] = n0.T.astype(BF).reshape(NZ, ROWS, D)
    zb[:, 1] = n1.T.astype(BF).reshape(NZ, ROWS, D)
    h0 = d0.astype(BF).astype(F32)
    h1 = d1.astype(BF).astype(F32)
    srow = lax.broadcasted_iota(jnp.int32, (16, D), 0)
    st = jnp.zeros((16, D), F32)
    for n, v in enumerate((t0, h0, d0 - h0, t1, h1, d1 - h1)):
        st = jnp.where(srow == n, v, st)
    st = st.astype(BF)
    for i in range(NZ):
        zb[i, 2] = st
    for i in range(1, NZ):
        push(zb.at[(z + i) % NZ], rz.at[i], 8, rp6.at[0], zpeer(i))
    rz[0] = zb[z]

    take(rsuf.at[0], 96)
    suffix = []
    for k in range(2):
        r = slice(ROWS * k, ROWS * (k + 1))
        tops = [sr[i, 1, r, 0:1] for i in range(4)]
        top = jnp.maximum(jnp.maximum(tops[0], tops[1]), jnp.maximum(tops[2], tops[3]))
        num = jnp.zeros((ROWS, D), F32)
        den = jnp.zeros((ROWS, 1), F32)
        for i in range(4):
            f = jnp.exp2((tops[i] - top) * C2)
            num = num + f * sr[i, 0, r, :]
            den = den + f * sr[i, 1, r, 1:2]
        suffix.append((num, top, den))

    take(rp6.at[0], 84)
    stats = [rz[i, 2].astype(F32) for i in range(NZ)]
    for k in range(2):
        tops = [s[3 * k : 3 * k + 1, :] for s in stats]
        top = tops[0]
        for t in tops[1:]:
            top = jnp.maximum(top, t)
        den = jnp.zeros((1, D), F32)
        for i in range(NZ):
            f = jnp.exp2((tops[i] - top) * C2)
            den = den + f * (stats[i][3 * k + 1 : 3 * k + 2, :] + stats[i][3 * k + 2 : 3 * k + 3, :])
            fs[16 * k + i : 16 * k + i + 1, :] = f
        fs[16 * k + 8 : 16 * k + 9, :] = top
        fs[16 * k + 9 : 16 * k + 10, :] = den
    ft[...] = fs[...].T
    own = ft[pl.ds(pl.multiple_of(z * ROWS, ROWS), ROWS), :]
    for k in range(2):
        num = jnp.zeros((ROWS, D), F32)
        for i in range(NZ):
            num = num + own[:, 16 * k + i : 16 * k + i + 1] * rz[i, k].astype(F32)
        top = own[:, 16 * k + 8 : 16 * k + 9]
        den = own[:, 16 * k + 9 : 16 * k + 10]
        snum, stop, sden = suffix[k]
        both = jnp.maximum(top, stop)
        f = jnp.exp2((top - both) * C2)
        g = jnp.exp2((stop - both) * C2)
        att = (num * f + snum * g) / (den * f + sden * g)
        for j in range(8):
            oscr[:, D * (8 * k + j) : D * (8 * k + j + 1)] = att[2 * j : 2 * j + 2, :]
    out_ref[...] = oscr[...].astype(BF)

    for phase, kib in enumerate((56, 24, 1024, 192, 768, 96, 936, 144, 84)):
        take(sent.at[phase], kib)


def body(queries, prefix_keys, prefix_values, branch_suffix_keys, suffix_values, lengths):
    dma = pltpu.SemaphoreType.DMA
    vmem = pltpu.VMEM
    scratch = [
        vmem((2, 2048), BF),
        vmem((32, D), F32),
        vmem((NZ, 2, ROWS, D), BF),
        vmem((4, 2, ROWS, D), BF),
        vmem((NY, 2, 2, NZ, ROWS, D), BF),
        vmem((NX, NY, NZ, ROWS, D), BF),
        vmem((2, 2 * SPAN, 256), BF),
        vmem((2, 2 * SPAN, 256), BF),
        vmem((2, 2, TILE, 2 * SPAN), BF),
        vmem((2, SPAN, 1024), BF),
        vmem((2, SPAN, 1024), BF),
        vmem((128, 1024), BF),
        vmem((2, 2 * SPAN, 256), F32),
        vmem((2, 2 * SPAN, 256), BF),
        vmem((256, 8, D), F32),
        vmem((4, 2, 2, TILE, D), BF),
        vmem((4, NY, TILE, D), BF),
        vmem((4, 4, TILE, D), BF),
        vmem((4, 4, TILE, D), BF),
        vmem((4, TILE, D), BF),
        vmem((4, TILE, D), BF),
        vmem((4, TILE, D), BF),
        vmem((4, TILE, D), BF),
        vmem((NZ, 3, ROWS, D), BF),
        vmem((NZ, 3, ROWS, D), BF),
        vmem((4, 2, 32, D), F32),
        vmem((4, 2, 32, D), F32),
        vmem((D, D), F32),
        vmem((D, D), F32),
        vmem((2, 2048), F32),
        dma((9,)),
        dma((1,)),
        dma((4,)),
        dma((2, 4)),
        dma((2, 4)),
        dma((2,)),
        dma((1,)),
        dma((1,)),
        dma((1,)),
        dma((1,)),
        dma((5,)),
    ]
    hbm = pl.BlockSpec(memory_space=pltpu.HBM)
    return pl.pallas_call(
        kernel,
        out_shape=jax.ShapeDtypeStruct((2, 2048), BF),
        in_specs=[
            pl.BlockSpec(memory_space=pltpu.SMEM),
            hbm, hbm, hbm, hbm, hbm,
        ],
        out_specs=pl.BlockSpec(memory_space=pltpu.VMEM),
        scratch_shapes=scratch,
        compiler_params=pltpu.CompilerParams(
            collective_id=0, has_side_effects=True, vmem_limit_bytes=60 * 1024 * 1024
        ),
        cost_estimate=pl.CostEstimate(flops=2_800_000_000, bytes_accessed=8_000_000, transcendentals=4_500_000),
        name="attend",
    )(lengths, queries, prefix_keys, prefix_values, branch_suffix_keys, suffix_values)


def solution(mesh):
    placed = (
        P("br", "ctx"),
        P(("ctx", "br"), None),
        P(("ctx", "br"), None),
        P("br", "ctx", None),
        P("br", "ctx", None),
        P("br"),
    )
    return jax.shard_map(
        body, mesh=mesh, in_specs=placed, out_specs=P("br", "ctx"), check_vma=False
    )
```

```python
import functools

import jax
import jax.numpy as jnp
from jax import lax
from jax.experimental import pallas as pl
from jax.experimental.pallas import tpu as pltpu
from jax.sharding import PartitionSpec as P

MESH = pl.DeviceIdType.MESH
BF = jnp.bfloat16
F32 = jnp.float32

D = 128
SPAN = 512
NX, NY, NZ = 4, 4, 8
ROWS = 16
TILE = 144
SCALE = D ** (-0.5)
LOG2E = 1.4426950408889634
C2 = SCALE * LOG2E
NEG = -1e30
LAST = 3
FAR = (4, 3, 5, 2, 6, 1, 7)
ACROSS = (2, 1, 3)
CHUNK = 256


def nt(a, b):
    return lax.dot_general(a, b, (((1,), (1,)), ((), ())), preferred_element_type=F32)


def pack(ref, numer, top, denom):
    row = lax.broadcasted_iota(jnp.int32, (16, top.shape[1]), 0)
    high = denom.astype(BF).astype(F32)
    low = denom - high
    stats = jnp.where(row == 0, top, jnp.where(row == 1, high, low))
    ref[0:D, :] = numer.astype(BF)
    ref[D:TILE, :] = stats.astype(BF)


def merge(refs):
    stats = [r[D:TILE, :].astype(F32) for r in refs]
    tops = [s[0:1, :] for s in stats]
    top = tops[0]
    for t in tops[1:]:
        top = jnp.maximum(top, t)
    numer, denom = None, None
    for r, s, t in zip(refs, stats, tops):
        factor = jnp.exp2((t - top) * C2)
        n = r[0:D, :].astype(F32) * factor
        d = (s[1:2, :] + s[2:3, :]) * factor
        numer = n if numer is None else numer + n
        denom = d if denom is None else denom + d
    return numer, top, denom


def kernel(
    len_ref, q_ref, pk, pv, sk, sv, out_ref,
    qraw, qscr, qz, qc, q0, q1, kbuf, vbuf, vt, skb, svb, qbd, ss, ps, pad,
    o0, o1, rx0, rx1, m0, m1, ry0, ry1, zb, rz, sb, sr, fs, ft, oscr,
    sent, rz1, rq2, rq3, rp4, rp5, rp6, rctx, rsuf, rkv, loc,
):
    c = lax.axis_index("ctx")
    br = lax.axis_index("br")
    core = c % 2
    xlo = c // 2
    z = br % NZ
    y = (br // NZ) % NY
    xhi = br // (NZ * NY)
    x = xhi * 2 + xlo

    def dev(px, py, pz, pc):
        return ((px % 2) * 2 + pc, (px // 2) * (NZ * NY) + py * NZ + pz)

    def xpeer(i):
        return dev((x + i) % NX, y, z, core)

    def ypeer(i):
        return dev(x, (y + i) % NY, z, core)

    def zpeer(i):
        return dev(x, y, (z + i) % NZ, core)

    def cpeer(i):
        return ((c + i) % 4, br)

    mate = dev(x, y, z, 1 - core)

    def remote(src, dst, ssem, rsem, who):
        return pltpu.make_async_remote_copy(
            src_ref=src, dst_ref=dst, send_sem=ssem, recv_sem=rsem, device_id=who, device_id_type=MESH
        )

    def push(src, dst, phase, rsem, who):
        remote(src, dst, sent.at[phase], rsem, who).start()

    def take(sem, kib):
        size = pad.at[0 : kib // 4]
        pltpu.make_async_copy(size, size, sem).wait()

    def load(src, dst, n):
        pltpu.make_async_copy(src, dst, loc.at[n]).start()

    def cols(a, k):
        return pl.ds(pl.multiple_of((a * 2 + k) * 256, 256), 256)

    barrier = pltpu.get_barrier_semaphore()
    peers = [zpeer(i) for i in FAR] + [ypeer(i) for i in ACROSS] + [xpeer(i) for i in ACROSS]
    peers += [mate, dev(x + 1 - 2 * xlo, y, z, 1 - core)]
    for who in peers:
        pl.semaphore_signal(barrier, inc=1, device_id=who, device_id_type=MESH)

    load(q_ref, qraw, 0)
    for a in range(2):
        load(pv.at[:, cols(a, core)], vbuf.at[a, 0:SPAN], 1)
        load(pk.at[:, cols(a, core)], kbuf.at[a, 0:SPAN], 2)
    load(sk, skb, 3)
    load(sv, svb, 4)

    pltpu.make_async_copy(qraw, qraw, loc.at[0]).wait()
    qf = qraw[...].astype(F32)
    for j in range(16):
        qscr[2 * j : 2 * j + 2, :] = qf[:, D * j : D * (j + 1)]
    for k in range(2):
        qk = qscr[ROWS * k : ROWS * (k + 1), :].astype(BF)
        qz[z, k] = qk
        qc[c, k] = qk

    qbd[...] = jnp.zeros_like(qbd)
    fs[...] = jnp.zeros_like(fs)

    def turn(a, k, part):
        vt[a, k, 0:D, SPAN * part : SPAN * (part + 1)] = vbuf[
            a, SPAN * part : SPAN * (part + 1), D * k : D * (k + 1)
        ].T

    take(loc.at[1], 512)
    for a in range(2):
        for k in range(2):
            turn(a, k, 0)
            vt[a, k, D:TILE, :] = jnp.ones((16, 2 * SPAN), BF)

    pl.semaphore_wait(barrier, len(peers))

    for i in FAR:
        push(qz.at[z], qz.at[z], 0, rz1.at[0], zpeer(i))
    for i in range(1, 4):
        push(qz.at[z], qc.at[c], 1, rctx.at[0], cpeer(i))
    for a in range(2):
        push(pk.at[:, cols(a, 1 - core)], kbuf.at[a, SPAN : 2 * SPAN], 2, rkv.at[0], mate)
        push(pv.at[:, cols(a, 1 - core)], vbuf.at[a, SPAN : 2 * SPAN], 2, rkv.at[0], mate)

    take(rz1.at[0], 56)

    for i in ACROSS:
        push(qz.at[:, 0], q0.at[y, xlo, xhi], 3, rq2.at[i], ypeer(i))
        push(qz.at[:, 1], q1.at[x, y], 3, rq2.at[i], xpeer(i))
    q0[y, xlo, xhi] = qz[:, 0]
    q1[x, y] = qz[:, 1]

    def forward(j):
        t0 = q0.at[(y + NY - j) % NY, xlo, xhi]
        t1 = q1.at[(x + NX - j) % NX, y]
        for i in ACROSS:
            push(t0, t0, 4, rq3.at[0, j], xpeer(i))
            push(t1, t1, 4, rq3.at[1, j], ypeer(i))

    forward(0)

    take(rctx.at[0], 24)
    for h in range(8):
        qbd[ROWS * h : ROWS * (h + 1), D * h : D * (h + 1)] = qc[h // 2, h % 2]
    pltpu.make_async_copy(skb, skb, loc.at[3]).wait()
    pltpu.make_async_copy(svb, svb, loc.at[4]).wait()
    raw = jnp.concatenate([nt(qbd[...], skb[0]), nt(qbd[...], skb[1])], axis=1)
    row = lax.broadcasted_iota(jnp.int32, (8 * ROWS, 2 * SPAN), 0)
    col = lax.broadcasted_iota(jnp.int32, (8 * ROWS, 2 * SPAN), 1)
    branch = col // SPAN
    live = (row % 2 == branch) & (c * SPAN + col % SPAN < jnp.where(branch == 0, len_ref[0], len_ref[1]))
    raw = jnp.where(live, raw, NEG)
    stop = jnp.max(raw, axis=1, keepdims=True)
    w = jnp.where(live, jnp.exp2((raw - stop) * C2), 0.0).astype(BF)
    sden = jnp.sum(w.astype(F32), axis=1, keepdims=True)
    snum = jnp.dot(w[:, :SPAN], svb[0], preferred_element_type=F32) + jnp.dot(
        w[:, SPAN:], svb[1], preferred_element_type=F32
    )
    lane = lax.broadcasted_iota(jnp.int32, (8 * ROWS, D), 1)
    sstat = jnp.where(lane == 0, stop, sden)
    for h in range(8):
        r = slice(ROWS * (h % 2), ROWS * (h % 2) + ROWS)
        sb[h // 2, 0, r, :] = snum[ROWS * h : ROWS * (h + 1), D * h : D * (h + 1)]
        sb[h // 2, 1, r, :] = sstat[ROWS * h : ROWS * (h + 1), :]
    for i in range(1, 4):
        push(sb.at[(c + i) % 4], sr.at[i], 5, rsuf.at[0], cpeer(i))
    sr[0] = sb[c]

    for j in range(1, 4):
        take(rq2.at[j], 64)
        forward(j)

    take(loc.at[2], 512)
    take(rkv.at[0], 1024)
    for a in range(2):
        for k in range(2):
            turn(a, k, 1)

    def attend(units, after):
        def score(u, n):
            a, k, q = units[u][:3]
            rows = slice(CHUNK * n, CHUNK * (n + 1))
            s = nt(kbuf[a, rows, D * k : D * (k + 1)], q)
            ss[u % 2, rows] = s
            return jnp.max(s, axis=0, keepdims=True)

        count = 2 * SPAN // CHUNK
        tops = [score(0, n) for n in range(count)]
        for u, (a, k, _, out_a, out_b) in enumerate(units):
            top = functools.reduce(jnp.maximum, tops).astype(BF).astype(F32)
            tops = []
            for n in range(count):
                if u + 1 < len(units):
                    tops.append(score(u + 1, n))
                rows = slice(CHUNK * n, CHUNK * (n + 1))
                ps[u % 2, rows] = jnp.exp2((ss[u % 2, rows] - top) * C2).astype(BF)
            n = jnp.dot(vt[a, k], ps[u % 2], preferred_element_type=F32)
            den = n[D : D + 1, :]
            pack(out_a, n[0:D, :D], top[:, :D], den[:, :D])
            pack(out_b, n[0:D, D:], top[:, D:], den[:, D:])
            after(u)

    def partial(j, i):
        px = (x + i) % NX
        py = (y + i) % NY
        mine0 = o0.at[j, px % 2, px // 2]
        mine1 = o1.at[j, py]
        if isinstance(j, int) and j == LAST:
            to0, to1 = dev(px, (y + NY - j) % NY, z, core), dev((x + NX - j) % NX, py, z, core)
        else:
            to0, to1 = xpeer(i), ypeer(i)
        return (
            remote(mine0, rx0.at[i, j], sent.at[6], rp4.at[0, j], to0),
            remote(mine1, rx1.at[i, j], sent.at[6], rp4.at[1, j], to1),
        )

    def reduce(j):
        take(rp4.at[0, j], 108)
        pack(m0.at[j], *merge([o0.at[j, xlo, xhi]] + [rx0.at[i, j] for i in range(1, 4)]))
        take(rp4.at[1, j], 108)
        pack(m1.at[j], *merge([o1.at[j, y]] + [rx1.at[i, j] for i in range(1, 4)]))

    def step(j, _):
        py = (y + NY - j) % NY
        px = (x + NX - j) % NX
        take(rq3.at[0, j], 96)
        take(rq3.at[1, j], 96)
        units = [(a, 0, q0[py, a].reshape(256, D), o0.at[j, a, 0], o0.at[j, a, 1]) for a in range(2)]
        for v in range(2):
            q = q1[px, 2 * v : 2 * v + 2].reshape(256, D)
            units.append((px % 2, 1, q, o1.at[j, 2 * v], o1.at[j, 2 * v + 1]))

        order = (2, 1, 3, 0) if isinstance(j, int) else ACROSS

        def after(u):
            if u % 2:
                for i in order:
                    partial(j, i)[u // 2].start()

        attend(units, after)

        @pl.when(j > 0)
        def _():
            reduce(j - 1)

        @pl.when(j > 1)
        def _():
            push(m0.at[j - 1], ry0.at[j - 1], 7, rp5.at[0], ypeer(NY - j + 1))
            push(m1.at[j - 1], ry1.at[j - 1], 7, rp5.at[1], xpeer(NX - j + 1))

        return 0

    lax.fori_loop(0, LAST, step, 0)
    step(LAST, 0)
    take(rp5.at[0], 72)
    take(rp4.at[0, LAST], 144)
    n0, t0, d0 = merge([m0.at[0], ry0.at[1], ry0.at[2]] + [rx0.at[i, LAST] for i in range(4)])
    take(rp5.at[1], 72)
    take(rp4.at[1, LAST], 144)
    n1, t1, d1 = merge([m1.at[0], ry1.at[1], ry1.at[2]] + [rx1.at[i, LAST] for i in range(4)])

    zb[:, 0] = n0.T.astype(BF).reshape(NZ, ROWS, D)
    zb[:, 1] = n1.T.astype(BF).reshape(NZ, ROWS, D)
    h0 = d0.astype(BF).astype(F32)
    h1 = d1.astype(BF).astype(F32)
    srow = lax.broadcasted_iota(jnp.int32, (16, D), 0)
    st = jnp.zeros((16, D), F32)
    for n, v in enumerate((t0, h0, d0 - h0, t1, h1, d1 - h1)):
        st = jnp.where(srow == n, v, st)
    st = st.astype(BF)
    for i in range(NZ):
        zb[i, 2] = st
    for i in FAR:
        push(zb.at[(z + i) % NZ], rz.at[i], 8, rp6.at[0], zpeer(i))
    rz[0] = zb[z]

    take(rsuf.at[0], 96)
    suffix = []
    for k in range(2):
        r = slice(ROWS * k, ROWS * (k + 1))
        tops = [sr[i, 1, r, 0:1] for i in range(4)]
        top = jnp.maximum(jnp.maximum(tops[0], tops[1]), jnp.maximum(tops[2], tops[3]))
        num = jnp.zeros((ROWS, D), F32)
        den = jnp.zeros((ROWS, 1), F32)
        for i in range(4):
            f = jnp.exp2((tops[i] - top) * C2)
            num = num + f * sr[i, 0, r, :]
            den = den + f * sr[i, 1, r, 1:2]
        suffix.append((num, top, den))

    take(rp6.at[0], 84)
    stats = [rz[i, 2].astype(F32) for i in range(NZ)]
    for k in range(2):
        tops = [s[3 * k : 3 * k + 1, :] for s in stats]
        top = tops[0]
        for t in tops[1:]:
            top = jnp.maximum(top, t)
        den = jnp.zeros((1, D), F32)
        for i in range(NZ):
            f = jnp.exp2((tops[i] - top) * C2)
            den = den + f * (stats[i][3 * k + 1 : 3 * k + 2, :] + stats[i][3 * k + 2 : 3 * k + 3, :])
            fs[16 * k + i : 16 * k + i + 1, :] = f
        fs[16 * k + 8 : 16 * k + 9, :] = top
        fs[16 * k + 9 : 16 * k + 10, :] = den
    ft[...] = fs[...].T
    own = ft[pl.ds(pl.multiple_of(z * ROWS, ROWS), ROWS), :]
    for k in range(2):
        num = jnp.zeros((ROWS, D), F32)
        for i in range(NZ):
            num = num + own[:, 16 * k + i : 16 * k + i + 1] * rz[i, k].astype(F32)
        top = own[:, 16 * k + 8 : 16 * k + 9]
        den = own[:, 16 * k + 9 : 16 * k + 10]
        snum, stop, sden = suffix[k]
        both = jnp.maximum(top, stop)
        f = jnp.exp2((top - both) * C2)
        g = jnp.exp2((stop - both) * C2)
        att = (num * f + snum * g) / (den * f + sden * g)
        for j in range(8):
            oscr[:, D * (8 * k + j) : D * (8 * k + j + 1)] = att[2 * j : 2 * j + 2, :]
    out_ref[...] = oscr[...].astype(BF)

    for phase, kib in enumerate((56, 24, 1024, 192, 768, 96, 936, 144, 84)):
        take(sent.at[phase], kib)


def body(queries, prefix_keys, prefix_values, branch_suffix_keys, suffix_values, lengths):
    dma = pltpu.SemaphoreType.DMA
    vmem = pltpu.VMEM
    scratch = [
        vmem((2, 2048), BF),
        vmem((32, D), F32),
        vmem((NZ, 2, ROWS, D), BF),
        vmem((4, 2, ROWS, D), BF),
        vmem((NY, 2, 2, NZ, ROWS, D), BF),
        vmem((NX, NY, NZ, ROWS, D), BF),
        vmem((2, 2 * SPAN, 256), BF),
        vmem((2, 2 * SPAN, 256), BF),
        vmem((2, 2, TILE, 2 * SPAN), BF),
        vmem((2, SPAN, 1024), BF),
        vmem((2, SPAN, 1024), BF),
        vmem((128, 1024), BF),
        vmem((2, 2 * SPAN, 256), F32),
        vmem((2, 2 * SPAN, 256), BF),
        vmem((256, 8, D), F32),
        vmem((4, 2, 2, TILE, D), BF),
        vmem((4, NY, TILE, D), BF),
        vmem((4, 4, TILE, D), BF),
        vmem((4, 4, TILE, D), BF),
        vmem((4, TILE, D), BF),
        vmem((4, TILE, D), BF),
        vmem((4, TILE, D), BF),
        vmem((4, TILE, D), BF),
        vmem((NZ, 3, ROWS, D), BF),
        vmem((NZ, 3, ROWS, D), BF),
        vmem((4, 2, 32, D), F32),
        vmem((4, 2, 32, D), F32),
        vmem((D, D), F32),
        vmem((D, D), F32),
        vmem((2, 2048), F32),
        dma((9,)),
        dma((1,)),
        dma((4,)),
        dma((2, 4)),
        dma((2, 4)),
        dma((2,)),
        dma((1,)),
        dma((1,)),
        dma((1,)),
        dma((1,)),
        dma((5,)),
    ]
    hbm = pl.BlockSpec(memory_space=pltpu.HBM)
    return pl.pallas_call(
        kernel,
        out_shape=jax.ShapeDtypeStruct((2, 2048), BF),
        in_specs=[
            pl.BlockSpec(memory_space=pltpu.SMEM),
            hbm, hbm, hbm, hbm, hbm,
        ],
        out_specs=pl.BlockSpec(memory_space=pltpu.VMEM),
        scratch_shapes=scratch,
        compiler_params=pltpu.CompilerParams(
            collective_id=0, has_side_effects=True, vmem_limit_bytes=60 * 1024 * 1024
        ),
        cost_estimate=pl.CostEstimate(flops=2_800_000_000, bytes_accessed=8_000_000, transcendentals=4_500_000),
        name="attend",
    )(lengths, queries, prefix_keys, prefix_values, branch_suffix_keys, suffix_values)


def solution(mesh):
    placed = (
        P("br", "ctx"),
        P(("ctx", "br"), None),
        P(("ctx", "br"), None),
        P("br", "ctx", None),
        P("br", "ctx", None),
        P("br"),
    )
    return jax.shard_map(
        body, mesh=mesh, in_specs=placed, out_specs=P("br", "ctx"), check_vma=False
    )
```

```python
import functools

import jax
import jax.numpy as jnp
from jax import lax
from jax.experimental import pallas as pl
from jax.experimental.pallas import tpu as pltpu
from jax.sharding import PartitionSpec as P

MESH = pl.DeviceIdType.MESH
BF = jnp.bfloat16
F32 = jnp.float32

D = 128
SPAN = 512
NX, NY, NZ = 4, 4, 8
ROWS = 16
TILE = 144
SCALE = D ** (-0.5)
LOG2E = 1.4426950408889634
C2 = SCALE * LOG2E
NEG = -1e30
LAST = 3
FAR = (4, 3, 5, 2, 6, 1, 7)
ACROSS = (2, 1, 3)
CHUNK = 256


def nt(a, b):
    return lax.dot_general(a, b, (((1,), (1,)), ((), ())), preferred_element_type=F32)


def pack(ref, numer, top, denom):
    row = lax.broadcasted_iota(jnp.int32, (16, top.shape[1]), 0)
    high = denom.astype(BF).astype(F32)
    low = denom - high
    stats = jnp.where(row == 0, top, jnp.where(row == 1, high, low))
    ref[0:D, :] = numer.astype(BF)
    ref[D:TILE, :] = stats.astype(BF)


def merge(refs):
    stats = [r[D:TILE, :].astype(F32) for r in refs]
    tops = [s[0:1, :] for s in stats]
    top = tops[0]
    for t in tops[1:]:
        top = jnp.maximum(top, t)
    numer, denom = None, None
    for r, s, t in zip(refs, stats, tops):
        factor = jnp.exp2((t - top) * C2)
        n = r[0:D, :].astype(F32) * factor
        d = (s[1:2, :] + s[2:3, :]) * factor
        numer = n if numer is None else numer + n
        denom = d if denom is None else denom + d
    return numer, top, denom


def kernel(
    len_ref, q_ref, pk, pv, sk, sv, out_ref,
    qraw, qscr, qz, qc, q0, q1, kbuf, vbuf, vt, skb, svb, qbd, ss, ps, pad,
    o0, o1, rx0, rx1, m0, m1, ry0, ry1, zb, rz, sb, sr, fs, ft, oscr,
    sent, rz1, rq2, rq3, rp4, rp5, rp6, rctx, rsuf, rkv, loc,
):
    c = lax.axis_index("ctx")
    br = lax.axis_index("br")
    core = c % 2
    xlo = c // 2
    z = br % NZ
    y = (br // NZ) % NY
    xhi = br // (NZ * NY)
    x = xhi * 2 + xlo

    def dev(px, py, pz, pc):
        return ((px % 2) * 2 + pc, (px // 2) * (NZ * NY) + py * NZ + pz)

    def xpeer(i):
        return dev((x + i) % NX, y, z, core)

    def ypeer(i):
        return dev(x, (y + i) % NY, z, core)

    def zpeer(i):
        return dev(x, y, (z + i) % NZ, core)

    def cpeer(i):
        return ((c + i) % 4, br)

    mate = dev(x, y, z, 1 - core)

    def remote(src, dst, ssem, rsem, who):
        return pltpu.make_async_remote_copy(
            src_ref=src, dst_ref=dst, send_sem=ssem, recv_sem=rsem, device_id=who, device_id_type=MESH
        )

    def push(src, dst, phase, rsem, who):
        remote(src, dst, sent.at[phase], rsem, who).start()

    def take(sem, kib):
        size = pad.at[0 : kib // 4]
        pltpu.make_async_copy(size, size, sem).wait()

    def load(src, dst, n):
        pltpu.make_async_copy(src, dst, loc.at[n]).start()

    def cols(a, k):
        return pl.ds(pl.multiple_of((a * 2 + k) * 256, 256), 256)

    barrier = pltpu.get_barrier_semaphore()
    peers = [zpeer(i) for i in FAR] + [ypeer(i) for i in ACROSS] + [xpeer(i) for i in ACROSS]
    peers += [mate, dev(x + 1 - 2 * xlo, y, z, 1 - core)]
    for who in peers:
        pl.semaphore_signal(barrier, inc=1, device_id=who, device_id_type=MESH)

    load(q_ref, qraw, 0)
    for a in range(2):
        load(pv.at[:, cols(a, core)], vbuf.at[a, 0:SPAN], 1)
        load(pk.at[:, cols(a, core)], kbuf.at[a, 0:SPAN], 2)
    load(sk, skb, 3)
    load(sv, svb, 4)

    pltpu.make_async_copy(qraw, qraw, loc.at[0]).wait()
    qf = qraw[...].astype(F32)
    for j in range(16):
        qscr[2 * j : 2 * j + 2, :] = qf[:, D * j : D * (j + 1)]
    for k in range(2):
        qk = qscr[ROWS * k : ROWS * (k + 1), :].astype(BF)
        qz[z, k] = qk
        qc[c, k] = qk

    qbd[...] = jnp.zeros_like(qbd)
    fs[...] = jnp.zeros_like(fs)

    def turn(a, k, part):
        vt[a, k, 0:D, SPAN * part : SPAN * (part + 1)] = vbuf[
            a, SPAN * part : SPAN * (part + 1), D * k : D * (k + 1)
        ].T

    take(loc.at[1], 512)
    for a in range(2):
        for k in range(2):
            turn(a, k, 0)
            vt[a, k, D:TILE, :] = jnp.ones((16, 2 * SPAN), BF)

    pl.semaphore_wait(barrier, len(peers))

    for i in FAR:
        push(qz.at[z], qz.at[z], 0, rz1.at[0], zpeer(i))
    for i in range(1, 4):
        push(qz.at[z], qc.at[c], 1, rctx.at[0], cpeer(i))
    for a in range(2):
        push(pk.at[:, cols(a, 1 - core)], kbuf.at[a, SPAN : 2 * SPAN], 2, rkv.at[0], mate)
        push(pv.at[:, cols(a, 1 - core)], vbuf.at[a, SPAN : 2 * SPAN], 2, rkv.at[0], mate)

    take(rz1.at[0], 56)

    for i in ACROSS:
        push(qz.at[:, 0], q0.at[y, xlo, xhi], 3, rq2.at[i], ypeer(i))
        push(qz.at[:, 1], q1.at[x, y], 3, rq2.at[i], xpeer(i))
    q0[y, xlo, xhi] = qz[:, 0]
    q1[x, y] = qz[:, 1]

    def forward(j):
        t0 = q0.at[(y + NY - j) % NY, xlo, xhi]
        t1 = q1.at[(x + NX - j) % NX, y]
        for i in ACROSS:
            push(t0, t0, 4, rq3.at[0, j], xpeer(i))
            push(t1, t1, 4, rq3.at[1, j], ypeer(i))

    forward(0)

    take(rctx.at[0], 24)
    for h in range(8):
        qbd[ROWS * h : ROWS * (h + 1), D * h : D * (h + 1)] = qc[h // 2, h % 2]
    pltpu.make_async_copy(skb, skb, loc.at[3]).wait()
    pltpu.make_async_copy(svb, svb, loc.at[4]).wait()
    raw = jnp.concatenate([nt(qbd[...], skb[0]), nt(qbd[...], skb[1])], axis=1)
    row = lax.broadcasted_iota(jnp.int32, (8 * ROWS, 2 * SPAN), 0)
    col = lax.broadcasted_iota(jnp.int32, (8 * ROWS, 2 * SPAN), 1)
    branch = col // SPAN
    live = (row % 2 == branch) & (c * SPAN + col % SPAN < jnp.where(branch == 0, len_ref[0], len_ref[1]))
    raw = jnp.where(live, raw, NEG)
    stop = jnp.max(raw, axis=1, keepdims=True)
    w = jnp.where(live, jnp.exp2((raw - stop) * C2), 0.0).astype(BF)
    sden = jnp.sum(w.astype(F32), axis=1, keepdims=True)
    snum = jnp.dot(w[:, :SPAN], svb[0], preferred_element_type=F32) + jnp.dot(
        w[:, SPAN:], svb[1], preferred_element_type=F32
    )
    lane = lax.broadcasted_iota(jnp.int32, (8 * ROWS, D), 1)
    sstat = jnp.where(lane == 0, stop, sden)
    for h in range(8):
        r = slice(ROWS * (h % 2), ROWS * (h % 2) + ROWS)
        sb[h // 2, 0, r, :] = snum[ROWS * h : ROWS * (h + 1), D * h : D * (h + 1)]
        sb[h // 2, 1, r, :] = sstat[ROWS * h : ROWS * (h + 1), :]
    for j in range(1, 4):
        take(rq2.at[j], 64)
        forward(j)

    take(loc.at[2], 512)
    take(rkv.at[0], 1024)
    for a in range(2):
        for k in range(2):
            turn(a, k, 1)

    def attend(units, after):
        def score(u, n):
            a, k, q = units[u][:3]
            rows = slice(CHUNK * n, CHUNK * (n + 1))
            s = nt(kbuf[a, rows, D * k : D * (k + 1)], q)
            ss[u % 2, rows] = s
            return jnp.max(s, axis=0, keepdims=True)

        count = 2 * SPAN // CHUNK
        tops = [score(0, n) for n in range(count)]
        for u, (a, k, _, out_a, out_b) in enumerate(units):
            top = functools.reduce(jnp.maximum, tops).astype(BF).astype(F32)
            tops = []
            for n in range(count):
                if u + 1 < len(units):
                    tops.append(score(u + 1, n))
                rows = slice(CHUNK * n, CHUNK * (n + 1))
                ps[u % 2, rows] = jnp.exp2((ss[u % 2, rows] - top) * C2).astype(BF)
            n = jnp.dot(vt[a, k], ps[u % 2], preferred_element_type=F32)
            den = n[D : D + 1, :]
            pack(out_a, n[0:D, :D], top[:, :D], den[:, :D])
            pack(out_b, n[0:D, D:], top[:, D:], den[:, D:])
            after(u)

    def partial(j, i):
        px = (x + i) % NX
        py = (y + i) % NY
        mine0 = o0.at[j, px % 2, px // 2]
        mine1 = o1.at[j, py]
        if isinstance(j, int) and j == LAST:
            to0, to1 = dev(px, (y + NY - j) % NY, z, core), dev((x + NX - j) % NX, py, z, core)
        else:
            to0, to1 = xpeer(i), ypeer(i)
        return (
            remote(mine0, rx0.at[i, j], sent.at[6], rp4.at[0, j], to0),
            remote(mine1, rx1.at[i, j], sent.at[6], rp4.at[1, j], to1),
        )

    def reduce(j):
        take(rp4.at[0, j], 108)
        pack(m0.at[j], *merge([o0.at[j, xlo, xhi]] + [rx0.at[i, j] for i in range(1, 4)]))
        take(rp4.at[1, j], 108)
        pack(m1.at[j], *merge([o1.at[j, y]] + [rx1.at[i, j] for i in range(1, 4)]))

    def step(j, _):
        py = (y + NY - j) % NY
        px = (x + NX - j) % NX
        take(rq3.at[0, j], 96)
        take(rq3.at[1, j], 96)
        units = [(a, 0, q0[py, a].reshape(256, D), o0.at[j, a, 0], o0.at[j, a, 1]) for a in range(2)]
        for v in range(2):
            q = q1[px, 2 * v : 2 * v + 2].reshape(256, D)
            units.append((px % 2, 1, q, o1.at[j, 2 * v], o1.at[j, 2 * v + 1]))

        order = (2, 1, 3, 0) if isinstance(j, int) else ACROSS

        def after(u):
            if u % 2:
                for i in order:
                    partial(j, i)[u // 2].start()

        attend(units, after)

        @pl.when(j > 0)
        def _():
            reduce(j - 1)

        @pl.when(j > 1)
        def _():
            push(m0.at[j - 1], ry0.at[j - 1], 7, rp5.at[0], ypeer(NY - j + 1))
            push(m1.at[j - 1], ry1.at[j - 1], 7, rp5.at[1], xpeer(NX - j + 1))

        return 0

    lax.fori_loop(0, LAST, step, 0)
    step(LAST, 0)
    for i in range(1, 4):
        push(sb.at[(c + i) % 4], sr.at[i], 5, rsuf.at[0], cpeer(i))
    sr[0] = sb[c]

    take(rp5.at[0], 72)
    take(rp4.at[0, LAST], 144)
    n0, t0, d0 = merge([m0.at[0], ry0.at[1], ry0.at[2]] + [rx0.at[i, LAST] for i in range(4)])
    take(rp5.at[1], 72)
    take(rp4.at[1, LAST], 144)
    n1, t1, d1 = merge([m1.at[0], ry1.at[1], ry1.at[2]] + [rx1.at[i, LAST] for i in range(4)])

    zb[:, 0] = n0.T.astype(BF).reshape(NZ, ROWS, D)
    zb[:, 1] = n1.T.astype(BF).reshape(NZ, ROWS, D)
    h0 = d0.astype(BF).astype(F32)
    h1 = d1.astype(BF).astype(F32)
    srow = lax.broadcasted_iota(jnp.int32, (16, D), 0)
    st = jnp.zeros((16, D), F32)
    for n, v in enumerate((t0, h0, d0 - h0, t1, h1, d1 - h1)):
        st = jnp.where(srow == n, v, st)
    st = st.astype(BF)
    for i in range(NZ):
        zb[i, 2] = st
    for i in FAR:
        push(zb.at[(z + i) % NZ], rz.at[i], 8, rp6.at[0], zpeer(i))
    rz[0] = zb[z]

    take(rsuf.at[0], 96)
    suffix = []
    for k in range(2):
        r = slice(ROWS * k, ROWS * (k + 1))
        tops = [sr[i, 1, r, 0:1] for i in range(4)]
        top = jnp.maximum(jnp.maximum(tops[0], tops[1]), jnp.maximum(tops[2], tops[3]))
        num = jnp.zeros((ROWS, D), F32)
        den = jnp.zeros((ROWS, 1), F32)
        for i in range(4):
            f = jnp.exp2((tops[i] - top) * C2)
            num = num + f * sr[i, 0, r, :]
            den = den + f * sr[i, 1, r, 1:2]
        suffix.append((num, top, den))

    take(rp6.at[0], 84)
    stats = [rz[i, 2].astype(F32) for i in range(NZ)]
    for k in range(2):
        tops = [s[3 * k : 3 * k + 1, :] for s in stats]
        top = tops[0]
        for t in tops[1:]:
            top = jnp.maximum(top, t)
        den = jnp.zeros((1, D), F32)
        for i in range(NZ):
            f = jnp.exp2((tops[i] - top) * C2)
            den = den + f * (stats[i][3 * k + 1 : 3 * k + 2, :] + stats[i][3 * k + 2 : 3 * k + 3, :])
            fs[16 * k + i : 16 * k + i + 1, :] = f
        fs[16 * k + 8 : 16 * k + 9, :] = top
        fs[16 * k + 9 : 16 * k + 10, :] = den
    ft[...] = fs[...].T
    own = ft[pl.ds(pl.multiple_of(z * ROWS, ROWS), ROWS), :]
    for k in range(2):
        num = jnp.zeros((ROWS, D), F32)
        for i in range(NZ):
            num = num + own[:, 16 * k + i : 16 * k + i + 1] * rz[i, k].astype(F32)
        top = own[:, 16 * k + 8 : 16 * k + 9]
        den = own[:, 16 * k + 9 : 16 * k + 10]
        snum, stop, sden = suffix[k]
        both = jnp.maximum(top, stop)
        f = jnp.exp2((top - both) * C2)
        g = jnp.exp2((stop - both) * C2)
        att = (num * f + snum * g) / (den * f + sden * g)
        for j in range(8):
            oscr[:, D * (8 * k + j) : D * (8 * k + j + 1)] = att[2 * j : 2 * j + 2, :]
    out_ref[...] = oscr[...].astype(BF)

    for phase, kib in enumerate((56, 24, 1024, 192, 768, 96, 936, 144, 84)):
        take(sent.at[phase], kib)


def body(queries, prefix_keys, prefix_values, branch_suffix_keys, suffix_values, lengths):
    dma = pltpu.SemaphoreType.DMA
    vmem = pltpu.VMEM
    scratch = [
        vmem((2, 2048), BF),
        vmem((32, D), F32),
        vmem((NZ, 2, ROWS, D), BF),
        vmem((4, 2, ROWS, D), BF),
        vmem((NY, 2, 2, NZ, ROWS, D), BF),
        vmem((NX, NY, NZ, ROWS, D), BF),
        vmem((2, 2 * SPAN, 256), BF),
        vmem((2, 2 * SPAN, 256), BF),
        vmem((2, 2, TILE, 2 * SPAN), BF),
        vmem((2, SPAN, 1024), BF),
        vmem((2, SPAN, 1024), BF),
        vmem((128, 1024), BF),
        vmem((2, 2 * SPAN, 256), F32),
        vmem((2, 2 * SPAN, 256), BF),
        vmem((256, 8, D), F32),
        vmem((4, 2, 2, TILE, D), BF),
        vmem((4, NY, TILE, D), BF),
        vmem((4, 4, TILE, D), BF),
        vmem((4, 4, TILE, D), BF),
        vmem((4, TILE, D), BF),
        vmem((4, TILE, D), BF),
        vmem((4, TILE, D), BF),
        vmem((4, TILE, D), BF),
        vmem((NZ, 3, ROWS, D), BF),
        vmem((NZ, 3, ROWS, D), BF),
        vmem((4, 2, 32, D), F32),
        vmem((4, 2, 32, D), F32),
        vmem((D, D), F32),
        vmem((D, D), F32),
        vmem((2, 2048), F32),
        dma((9,)),
        dma((1,)),
        dma((4,)),
        dma((2, 4)),
        dma((2, 4)),
        dma((2,)),
        dma((1,)),
        dma((1,)),
        dma((1,)),
        dma((1,)),
        dma((5,)),
    ]
    hbm = pl.BlockSpec(memory_space=pltpu.HBM)
    return pl.pallas_call(
        kernel,
        out_shape=jax.ShapeDtypeStruct((2, 2048), BF),
        in_specs=[
            pl.BlockSpec(memory_space=pltpu.SMEM),
            hbm, hbm, hbm, hbm, hbm,
        ],
        out_specs=pl.BlockSpec(memory_space=pltpu.VMEM),
        scratch_shapes=scratch,
        compiler_params=pltpu.CompilerParams(
            collective_id=0, has_side_effects=True, vmem_limit_bytes=60 * 1024 * 1024
        ),
        cost_estimate=pl.CostEstimate(flops=2_800_000_000, bytes_accessed=8_000_000, transcendentals=4_500_000),
        name="attend",
    )(lengths, queries, prefix_keys, prefix_values, branch_suffix_keys, suffix_values)


def solution(mesh):
    placed = (
        P("br", "ctx"),
        P(("ctx", "br"), None),
        P(("ctx", "br"), None),
        P("br", "ctx", None),
        P("br", "ctx", None),
        P("br"),
    )
    return jax.shard_map(
        body, mesh=mesh, in_specs=placed, out_specs=P("br", "ctx"), check_vma=False
    )
```

```python
import functools

import jax
import jax.numpy as jnp
from jax import lax
from jax.experimental import pallas as pl
from jax.experimental.pallas import tpu as pltpu
from jax.sharding import PartitionSpec as P

MESH = pl.DeviceIdType.MESH
BF = jnp.bfloat16
F32 = jnp.float32

D = 128
SPAN = 512
NX, NY, NZ = 4, 4, 8
ROWS = 16
TILE = 144
SCALE = D ** (-0.5)
LOG2E = 1.4426950408889634
C2 = SCALE * LOG2E
NEG = -1e30
LAST = 3
FAR = (4, 3, 5, 2, 6, 1, 7)
ACROSS = (2, 1, 3)
CHUNK = 256


def nt(a, b):
    return lax.dot_general(a, b, (((1,), (1,)), ((), ())), preferred_element_type=F32)


def pack(ref, numer, top, denom):
    row = lax.broadcasted_iota(jnp.int32, (16, top.shape[1]), 0)
    high = denom.astype(BF).astype(F32)
    low = denom - high
    stats = jnp.where(row == 0, top, jnp.where(row == 1, high, low))
    ref[0:D, :] = numer.astype(BF)
    ref[D:TILE, :] = stats.astype(BF)


def merge(refs):
    stats = [r[D:TILE, :].astype(F32) for r in refs]
    tops = [s[0:1, :] for s in stats]
    top = tops[0]
    for t in tops[1:]:
        top = jnp.maximum(top, t)
    numer, denom = None, None
    for r, s, t in zip(refs, stats, tops):
        factor = jnp.exp2((t - top) * C2)
        n = r[0:D, :].astype(F32) * factor
        d = (s[1:2, :] + s[2:3, :]) * factor
        numer = n if numer is None else numer + n
        denom = d if denom is None else denom + d
    return numer, top, denom


def kernel(
    len_ref, q_ref, pk, pv, sk, sv, out_ref,
    qraw, qscr, qz, qc, q0, q1, kbuf, vbuf, vt, skb, svb, qbd, ss, ps, pad,
    o0, o1, rx0, rx1, m0, m1, ry0, ry1, zb, rz, sb, sr, fs, ft, oscr,
    sent, rz1, rq2, rq3, rp4, rp5, rp6, rctx, rsuf, rkv, loc,
):
    c = lax.axis_index("ctx")
    br = lax.axis_index("br")
    core = c % 2
    xlo = c // 2
    z = br % NZ
    y = (br // NZ) % NY
    xhi = br // (NZ * NY)
    x = xhi * 2 + xlo

    def dev(px, py, pz, pc):
        return ((px % 2) * 2 + pc, (px // 2) * (NZ * NY) + py * NZ + pz)

    def xpeer(i):
        return dev((x + i) % NX, y, z, core)

    def ypeer(i):
        return dev(x, (y + i) % NY, z, core)

    def zpeer(i):
        return dev(x, y, (z + i) % NZ, core)

    def cpeer(i):
        return ((c + i) % 4, br)

    mate = dev(x, y, z, 1 - core)

    def remote(src, dst, ssem, rsem, who):
        return pltpu.make_async_remote_copy(
            src_ref=src, dst_ref=dst, send_sem=ssem, recv_sem=rsem, device_id=who, device_id_type=MESH
        )

    def push(src, dst, phase, rsem, who):
        remote(src, dst, sent.at[phase], rsem, who).start()

    def take(sem, kib):
        size = pad.at[0 : kib // 4]
        pltpu.make_async_copy(size, size, sem).wait()

    def load(src, dst, n):
        pltpu.make_async_copy(src, dst, loc.at[n]).start()

    def cols(a, k):
        return pl.ds(pl.multiple_of((a * 2 + k) * 256, 256), 256)

    barrier = pltpu.get_barrier_semaphore()
    peers = [zpeer(i) for i in FAR] + [ypeer(i) for i in ACROSS] + [xpeer(i) for i in ACROSS]
    peers += [mate, dev(x + 1 - 2 * xlo, y, z, 1 - core)]
    for who in peers:
        pl.semaphore_signal(barrier, inc=1, device_id=who, device_id_type=MESH)

    load(q_ref, qraw, 0)
    for a in range(2):
        load(pv.at[:, cols(a, core)], vbuf.at[a, 0:SPAN], 1)
        load(pk.at[:, cols(a, core)], kbuf.at[a, 0:SPAN], 2)
    load(sk, skb, 3)
    load(sv, svb, 4)

    pltpu.make_async_copy(qraw, qraw, loc.at[0]).wait()
    qf = qraw[...].astype(F32)
    for j in range(16):
        qscr[2 * j : 2 * j + 2, :] = qf[:, D * j : D * (j + 1)]
    for k in range(2):
        qk = qscr[ROWS * k : ROWS * (k + 1), :].astype(BF)
        qz[z, k] = qk
        qc[c, k] = qk

    qbd[...] = jnp.zeros_like(qbd)
    fs[...] = jnp.zeros_like(fs)

    def turn(a, k, part):
        vt[a, k, 0:D, SPAN * part : SPAN * (part + 1)] = vbuf[
            a, SPAN * part : SPAN * (part + 1), D * k : D * (k + 1)
        ].T

    take(loc.at[1], 512)
    for a in range(2):
        for k in range(2):
            turn(a, k, 0)
            vt[a, k, D:TILE, :] = jnp.ones((16, 2 * SPAN), BF)

    pl.semaphore_wait(barrier, len(peers))

    for a in range(2):
        push(pk.at[:, cols(a, 1 - core)], kbuf.at[a, SPAN : 2 * SPAN], 2, rkv.at[0], mate)
        push(pv.at[:, cols(a, 1 - core)], vbuf.at[a, SPAN : 2 * SPAN], 2, rkv.at[0], mate)
    for i in FAR:
        push(qz.at[z], qz.at[z], 0, rz1.at[0], zpeer(i))
    for i in range(1, 4):
        push(qz.at[z], qc.at[c], 1, rctx.at[0], cpeer(i))

    take(rz1.at[0], 56)

    for i in ACROSS:
        push(qz.at[:, 0], q0.at[y, xlo, xhi], 3, rq2.at[0, i], ypeer(i))
        push(qz.at[:, 1], q1.at[x, y], 3, rq2.at[1, i], xpeer(i))
    q0[y, xlo, xhi] = qz[:, 0]
    q1[x, y] = qz[:, 1]

    def forward0(j):
        part = q0.at[(y + NY - j) % NY, xlo, xhi]
        for i in ACROSS:
            push(part, part, 4, rq3.at[0, j], xpeer(i))

    def forward1(j):
        part = q1.at[(x + NX - j) % NX, y]
        for i in ACROSS:
            push(part, part, 4, rq3.at[1, j], ypeer(i))

    forward0(0)
    forward1(0)

    take(rctx.at[0], 24)
    for h in range(8):
        qbd[ROWS * h : ROWS * (h + 1), D * h : D * (h + 1)] = qc[h // 2, h % 2]
    pltpu.make_async_copy(skb, skb, loc.at[3]).wait()
    pltpu.make_async_copy(svb, svb, loc.at[4]).wait()
    raw = jnp.concatenate([nt(qbd[...], skb[0]), nt(qbd[...], skb[1])], axis=1)
    row = lax.broadcasted_iota(jnp.int32, (8 * ROWS, 2 * SPAN), 0)
    col = lax.broadcasted_iota(jnp.int32, (8 * ROWS, 2 * SPAN), 1)
    branch = col // SPAN
    live = (row % 2 == branch) & (c * SPAN + col % SPAN < jnp.where(branch == 0, len_ref[0], len_ref[1]))
    raw = jnp.where(live, raw, NEG)
    stop = jnp.max(raw, axis=1, keepdims=True)
    w = jnp.where(live, jnp.exp2((raw - stop) * C2), 0.0).astype(BF)
    sden = jnp.sum(w.astype(F32), axis=1, keepdims=True)
    snum = jnp.dot(w[:, :SPAN], svb[0], preferred_element_type=F32) + jnp.dot(
        w[:, SPAN:], svb[1], preferred_element_type=F32
    )
    lane = lax.broadcasted_iota(jnp.int32, (8 * ROWS, D), 1)
    sstat = jnp.where(lane == 0, stop, sden)
    for h in range(8):
        r = slice(ROWS * (h % 2), ROWS * (h % 2) + ROWS)
        sb[h // 2, 0, r, :] = snum[ROWS * h : ROWS * (h + 1), D * h : D * (h + 1)]
        sb[h // 2, 1, r, :] = sstat[ROWS * h : ROWS * (h + 1), :]
    for j in range(1, 4):
        take(rq2.at[0, j], 32)
        forward0(j)
        take(rq2.at[1, j], 32)
        forward1(j)

    take(loc.at[2], 512)
    take(rkv.at[0], 1024)
    for a in range(2):
        for k in range(2):
            turn(a, k, 1)

    def attend(units, after):
        def score(u, n):
            a, k, q = units[u][:3]
            rows = slice(CHUNK * n, CHUNK * (n + 1))
            s = nt(kbuf[a, rows, D * k : D * (k + 1)], q)
            ss[u % 2, rows] = s
            return jnp.max(s, axis=0, keepdims=True)

        count = 2 * SPAN // CHUNK
        tops = [score(0, n) for n in range(count)]
        for u, (a, k, _, out_a, out_b) in enumerate(units):
            top = functools.reduce(jnp.maximum, tops).astype(BF).astype(F32)
            tops = []
            for n in range(count):
                if u + 1 < len(units):
                    tops.append(score(u + 1, n))
                rows = slice(CHUNK * n, CHUNK * (n + 1))
                ps[u % 2, rows] = jnp.exp2((ss[u % 2, rows] - top) * C2).astype(BF)
            n = jnp.dot(vt[a, k], ps[u % 2], preferred_element_type=F32)
            den = n[D : D + 1, :]
            pack(out_a, n[0:D, :D], top[:, :D], den[:, :D])
            pack(out_b, n[0:D, D:], top[:, D:], den[:, D:])
            after(u)

    def partial(j, i):
        px = (x + i) % NX
        py = (y + i) % NY
        mine0 = o0.at[j, px % 2, px // 2]
        mine1 = o1.at[j, py]
        if isinstance(j, int) and j == LAST:
            to0, to1 = dev(px, (y + NY - j) % NY, z, core), dev((x + NX - j) % NX, py, z, core)
        else:
            to0, to1 = xpeer(i), ypeer(i)
        return (
            remote(mine0, rx0.at[i, j], sent.at[6], rp4.at[0, j], to0),
            remote(mine1, rx1.at[i, j], sent.at[6], rp4.at[1, j], to1),
        )

    def reduce(j):
        take(rp4.at[0, j], 108)
        pack(m0.at[j], *merge([o0.at[j, xlo, xhi]] + [rx0.at[i, j] for i in range(1, 4)]))
        onward = j > 0

        @pl.when(onward)
        def _():
            push(m0.at[j], ry0.at[j], 7, rp5.at[0], ypeer(NY - j))

        take(rp4.at[1, j], 108)
        pack(m1.at[j], *merge([o1.at[j, y]] + [rx1.at[i, j] for i in range(1, 4)]))

        @pl.when(onward)
        def _():
            push(m1.at[j], ry1.at[j], 7, rp5.at[1], xpeer(NX - j))

    def step(j, _):
        py = (y + NY - j) % NY
        px = (x + NX - j) % NX
        take(rq3.at[0, j], 96)
        take(rq3.at[1, j], 96)
        units = [(a, 0, q0[py, a].reshape(256, D), o0.at[j, a, 0], o0.at[j, a, 1]) for a in range(2)]
        for v in range(2):
            q = q1[px, 2 * v : 2 * v + 2].reshape(256, D)
            units.append((px % 2, 1, q, o1.at[j, 2 * v], o1.at[j, 2 * v + 1]))

        order = (2, 1, 3, 0) if isinstance(j, int) else ACROSS

        def after(u):
            if u % 2:
                for i in order:
                    partial(j, i)[u // 2].start()

        attend(units, after)

        @pl.when(j > 0)
        def _():
            reduce(j - 1)

        return 0

    lax.fori_loop(0, LAST, step, 0)
    step(LAST, 0)
    for i in range(1, 4):
        push(sb.at[(c + i) % 4], sr.at[i], 5, rsuf.at[0], cpeer(i))
    sr[0] = sb[c]

    take(rp5.at[0], 72)
    take(rp4.at[0, LAST], 144)
    n0, t0, d0 = merge([m0.at[0], ry0.at[1], ry0.at[2]] + [rx0.at[i, LAST] for i in range(4)])
    take(rp5.at[1], 72)
    take(rp4.at[1, LAST], 144)
    n1, t1, d1 = merge([m1.at[0], ry1.at[1], ry1.at[2]] + [rx1.at[i, LAST] for i in range(4)])

    zb[:, 0] = n0.T.astype(BF).reshape(NZ, ROWS, D)
    zb[:, 1] = n1.T.astype(BF).reshape(NZ, ROWS, D)
    h0 = d0.astype(BF).astype(F32)
    h1 = d1.astype(BF).astype(F32)
    srow = lax.broadcasted_iota(jnp.int32, (16, D), 0)
    st = jnp.zeros((16, D), F32)
    for n, v in enumerate((t0, h0, d0 - h0, t1, h1, d1 - h1)):
        st = jnp.where(srow == n, v, st)
    st = st.astype(BF)
    for i in range(NZ):
        zb[i, 2] = st
    for i in FAR:
        push(zb.at[(z + i) % NZ], rz.at[i], 8, rp6.at[0], zpeer(i))
    rz[0] = zb[z]

    take(rsuf.at[0], 96)
    suffix = []
    for k in range(2):
        r = slice(ROWS * k, ROWS * (k + 1))
        tops = [sr[i, 1, r, 0:1] for i in range(4)]
        top = jnp.maximum(jnp.maximum(tops[0], tops[1]), jnp.maximum(tops[2], tops[3]))
        num = jnp.zeros((ROWS, D), F32)
        den = jnp.zeros((ROWS, 1), F32)
        for i in range(4):
            f = jnp.exp2((tops[i] - top) * C2)
            num = num + f * sr[i, 0, r, :]
            den = den + f * sr[i, 1, r, 1:2]
        suffix.append((num, top, den))

    take(rp6.at[0], 84)
    stats = [rz[i, 2].astype(F32) for i in range(NZ)]
    for k in range(2):
        tops = [s[3 * k : 3 * k + 1, :] for s in stats]
        top = tops[0]
        for t in tops[1:]:
            top = jnp.maximum(top, t)
        den = jnp.zeros((1, D), F32)
        for i in range(NZ):
            f = jnp.exp2((tops[i] - top) * C2)
            den = den + f * (stats[i][3 * k + 1 : 3 * k + 2, :] + stats[i][3 * k + 2 : 3 * k + 3, :])
            fs[16 * k + i : 16 * k + i + 1, :] = f
        fs[16 * k + 8 : 16 * k + 9, :] = top
        fs[16 * k + 9 : 16 * k + 10, :] = den
    ft[...] = fs[...].T
    own = ft[pl.ds(pl.multiple_of(z * ROWS, ROWS), ROWS), :]
    for k in range(2):
        num = jnp.zeros((ROWS, D), F32)
        for i in range(NZ):
            num = num + own[:, 16 * k + i : 16 * k + i + 1] * rz[i, k].astype(F32)
        top = own[:, 16 * k + 8 : 16 * k + 9]
        den = own[:, 16 * k + 9 : 16 * k + 10]
        snum, stop, sden = suffix[k]
        both = jnp.maximum(top, stop)
        f = jnp.exp2((top - both) * C2)
        g = jnp.exp2((stop - both) * C2)
        att = (num * f + snum * g) / (den * f + sden * g)
        for j in range(8):
            oscr[:, D * (8 * k + j) : D * (8 * k + j + 1)] = att[2 * j : 2 * j + 2, :]
    out_ref[...] = oscr[...].astype(BF)

    for phase, kib in enumerate((56, 24, 1024, 192, 768, 96, 936, 144, 84)):
        take(sent.at[phase], kib)


def body(queries, prefix_keys, prefix_values, branch_suffix_keys, suffix_values, lengths):
    dma = pltpu.SemaphoreType.DMA
    vmem = pltpu.VMEM
    scratch = [
        vmem((2, 2048), BF),
        vmem((32, D), F32),
        vmem((NZ, 2, ROWS, D), BF),
        vmem((4, 2, ROWS, D), BF),
        vmem((NY, 2, 2, NZ, ROWS, D), BF),
        vmem((NX, NY, NZ, ROWS, D), BF),
        vmem((2, 2 * SPAN, 256), BF),
        vmem((2, 2 * SPAN, 256), BF),
        vmem((2, 2, TILE, 2 * SPAN), BF),
        vmem((2, SPAN, 1024), BF),
        vmem((2, SPAN, 1024), BF),
        vmem((128, 1024), BF),
        vmem((2, 2 * SPAN, 256), F32),
        vmem((2, 2 * SPAN, 256), BF),
        vmem((256, 8, D), F32),
        vmem((4, 2, 2, TILE, D), BF),
        vmem((4, NY, TILE, D), BF),
        vmem((4, 4, TILE, D), BF),
        vmem((4, 4, TILE, D), BF),
        vmem((4, TILE, D), BF),
        vmem((4, TILE, D), BF),
        vmem((4, TILE, D), BF),
        vmem((4, TILE, D), BF),
        vmem((NZ, 3, ROWS, D), BF),
        vmem((NZ, 3, ROWS, D), BF),
        vmem((4, 2, 32, D), F32),
        vmem((4, 2, 32, D), F32),
        vmem((D, D), F32),
        vmem((D, D), F32),
        vmem((2, 2048), F32),
        dma((9,)),
        dma((1,)),
        dma((2, 4)),
        dma((2, 4)),
        dma((2, 4)),
        dma((2,)),
        dma((1,)),
        dma((1,)),
        dma((1,)),
        dma((1,)),
        dma((5,)),
    ]
    hbm = pl.BlockSpec(memory_space=pltpu.HBM)
    return pl.pallas_call(
        kernel,
        out_shape=jax.ShapeDtypeStruct((2, 2048), BF),
        in_specs=[
            pl.BlockSpec(memory_space=pltpu.SMEM),
            hbm, hbm, hbm, hbm, hbm,
        ],
        out_specs=pl.BlockSpec(memory_space=pltpu.VMEM),
        scratch_shapes=scratch,
        compiler_params=pltpu.CompilerParams(
            collective_id=0, has_side_effects=True, vmem_limit_bytes=60 * 1024 * 1024
        ),
        cost_estimate=pl.CostEstimate(flops=2_800_000_000, bytes_accessed=8_000_000, transcendentals=4_500_000),
        name="attend",
    )(lengths, queries, prefix_keys, prefix_values, branch_suffix_keys, suffix_values)


def solution(mesh):
    placed = (
        P("br", "ctx"),
        P(("ctx", "br"), None),
        P(("ctx", "br"), None),
        P("br", "ctx", None),
        P("br", "ctx", None),
        P("br"),
    )
    return jax.shard_map(
        body, mesh=mesh, in_specs=placed, out_specs=P("br", "ctx"), check_vma=False
    )
```
